128 devices in a mesh: row: 16 (over x, y), vec: 8 (over z, core).
Axes of the slice: x: 4, y: 4, z: 4, core: 2. Of those that a mesh axis runs over, the one named last changes fastest.
Arguments:
- ham_tiles: bfloat16 [1024, 4, 128, 128], P('row'), may hold values from -0.125 to 0.125
- tile_columns: int32 [1024, 4], P('row'), may hold values from 0 to 1023, as said below
- stack_lengths: int32 [16], P('row'), may hold values from 32 to 64, as said below
- start_vectors: bfloat16 [131072, 1024], P('row', 'vec'), may hold values from -6 to 6
- spectral_scale: float32 [1], replicated, may hold values from 4 to 16
Outputs:
- filtered_basis: bfloat16 [131072, 1024], P('row', 'vec')
The draws below stay inside these ranges and needn't reach their ends.
Inputs may be any that keep to these rules, and one draw needn't show every extreme that they name: `tile_columns`: row b lists 4 distinct block columns; the first is b itself, the others are (b + o) mod 1024 with nonzero offsets o from -2 to 2. Some stack holds 64 occupied block rows and some other stack exactly half of 64; a stack's occupied rows are its first stack_lengths - 2 and its last 2 block rows.
All inputs are finite; a program needn't handle non-finite values.
Results may differ from the reference program's by a relative error of at most 0.006.
The reference program's roundings to bfloat16 on the way count: a program that leaves them out, or rounds other values in their place, can miss the bound.
Values may be sent and summed in bfloat16 or wider, within the bound.
No kernel may reach another device: no remote copies, remote signals or barrier semaphores. Data moves between devices by JAX's collectives and lax.ppermute only.
A program may use at most 128 MiB of HBM per device.

```python
import math
import jax
import jax.numpy as jnp
from jax import lax

TILE = 128
NT = 4
REACH = 2
M = 1024
CHEB = 6
NS_ITERS = 2
BLK_DEV = 64
STACKS = 16
NB = 1024
NR = 131072


def draw_tile_columns(key, part):
    block_ids = jnp.arange(NB, dtype=jnp.int32)
    offset_pool = jnp.array([-2, -1, 1, 2], dtype=jnp.int32)
    scores = jax.random.randint(key, (NB, 4), 0, 4096) * 4 + jnp.arange(4, dtype=jnp.int32)[None, :]
    ranking = jnp.argsort(scores, axis=1)
    chosen = offset_pool[ranking[:, :NT - 1]]
    offsets = jnp.concatenate([jnp.zeros((NB, 1), jnp.int32), chosen], axis=1)
    return ((block_ids[:, None] + offsets) % NB).astype(jnp.int32)


def draw_stack_lengths(key, part):
    key_full, key_uneven, key_first, key_second = jax.random.split(key, 4)
    full_flags = jax.random.randint(key_full, (STACKS,), 0, 2)
    uneven = jax.random.randint(key_uneven, (STACKS,), BLK_DEV // 2, BLK_DEV)
    counts = jnp.where(full_flags == 1, BLK_DEV, uneven)
    first_stack = jax.random.randint(key_first, (), 0, STACKS)
    second_stack = (first_stack + 1 + jax.random.randint(key_second, (), 0, STACKS - 1)) % STACKS
    counts = counts.at[first_stack].set(BLK_DEV).at[second_stack].set(BLK_DEV // 2)
    return counts.astype(jnp.int32)


def draw_start_vectors(key, part):
    key_entries = jax.random.fold_in(key, 71)
    values = jnp.clip(jax.random.normal(key_entries, (NR, M), jnp.float32), -6.0, 6.0)
    return values.astype(jnp.bfloat16)


def level_of(key, dims, cuts, least, top_value):
    def one(dim, parts):
        steps = jax.random.uniform(jax.random.fold_in(jax.random.fold_in(key, 6), dim), (parts,), jnp.float32, least / len(cuts), top_value / len(cuts))
        return jnp.repeat(jnp.exp(steps), dims[dim] // parts).reshape((-1,) + (1,) * (len(dims) - dim - 1))

    loudness = one(*cuts[0])
    for cut in cuts[1:]:
        loudness = loudness * one(*cut)
    return loudness


def gaussian(key, dims, spread, most, pieces=(), kind=jnp.bfloat16):
    values = spread * jax.random.normal(key, dims, jnp.float32)
    if pieces:
        values = values * level_of(key, dims, pieces, -0.22, 0.18)
    return jnp.clip(values, -most, most).astype(kind)


def setup_inputs(seed: int = 0) -> dict:
    keys = jax.random.split(jax.random.key(seed), 6)
    return {
        "ham_tiles": gaussian(keys[0], (NB, NT, TILE, TILE), (4 * NT * TILE) ** -0.5, 0.125, ((0, 16),)),
        "tile_columns": draw_tile_columns(jax.random.fold_in(keys[5], 71), 0),
        "stack_lengths": draw_stack_lengths(jax.random.fold_in(keys[5], 71), 0),
        "start_vectors": draw_start_vectors(jax.random.fold_in(keys[5], 71), 0),
        "spectral_scale": jnp.clip(jnp.exp(jax.random.uniform(keys[4], (1,), jnp.float32, math.log(4.0), math.log(16.0))), 4.0, 16.0),
    }


def apply_hamiltonian(ham_tiles, tile_columns, stack_lengths, current):
    blocked = current.reshape(NB, TILE, M)

    def group_product(group):
        start = (group * BLK_DEV).astype(jnp.int32)
        tile_group = lax.dynamic_slice_in_dim(ham_tiles, start, BLK_DEV, 0).astype(jnp.float32)
        column_group = lax.dynamic_slice_in_dim(tile_columns, start, BLK_DEV, 0)
        picked = blocked[column_group].astype(jnp.float32)
        product = jnp.einsum('btij,btjc->bic', tile_group, picked)
        local_rows = jnp.arange(BLK_DEV, dtype=jnp.int32)
        live = (local_rows < stack_lengths[group] - REACH) | (local_rows >= BLK_DEV - REACH)
        live_rows = live.astype(jnp.float32)
        return product * live_rows[:, None, None]
    stacked = lax.map(group_product, jnp.arange(STACKS, dtype=jnp.int32))
    return stacked.reshape(NR, M)

def reference(ham_tiles, tile_columns, stack_lengths, start_vectors, spectral_scale):
    earlier = start_vectors
    current = apply_hamiltonian(ham_tiles, tile_columns, stack_lengths, start_vectors).astype(jnp.bfloat16)
    for repeat in range(CHEB - 1):
        image = apply_hamiltonian(ham_tiles, tile_columns, stack_lengths, current)
        following = (2.0 * image - earlier.astype(jnp.float32)).astype(jnp.bfloat16)
        earlier, current = (current, following)
    filtered = current.astype(jnp.float32)
    gram = lax.dot_general(filtered, filtered, (((0,), (0,)), ((), ())), precision=lax.Precision.HIGHEST) / NR
    scale = spectral_scale[0] * jnp.trace(gram) / M
    system = gram / scale
    root = jnp.eye(M, dtype=jnp.float32)
    for repeat in range(NS_ITERS):
        product_w = jnp.dot(system, root, precision=lax.Precision.HIGHEST)
        product_p = jnp.dot(product_w, root, precision=lax.Precision.HIGHEST)
        root = 1.5 * root - 0.5 * jnp.dot(product_p, root, precision=lax.Precision.HIGHEST)
    weights = (root / jnp.sqrt(scale)).astype(jnp.bfloat16)
    basis = jnp.dot(filtered, weights.astype(jnp.float32), precision=lax.Precision.HIGHEST)
    return basis.astype(jnp.bfloat16)
```

```python
import functools

import jax
import jax.numpy as jnp
from jax import lax
from jax.experimental import pallas as pl
from jax.experimental.pallas import tpu as pltpu
from jax.sharding import PartitionSpec as P

REACH = 2
CHEB = 6
DEEP = REACH * CHEB
UNROLL = 4
BF = jnp.bfloat16
F32 = jnp.float32
ANY = pl.BlockSpec(memory_space=pl.ANY)
SMEM = pl.BlockSpec(memory_space=pltpu.SMEM)
VMEM = pl.BlockSpec(memory_space=pltpu.VMEM)


def filter_steps(count, row_shift, ids, live, tiles, first, even, odd, out, out_at):
    for step in range(1, CHEB + 1):
        source = first if step == 1 else (odd if step % 2 == 0 else even)
        target = odd if step % 2 else even
        before = first if step == 2 else target
        low = REACH * step

        def body(turn, carry, step=step, source=source, target=target, before=before, low=low):
            for part in range(UNROLL):
                block = low + turn * UNROLL + part
                row = block - row_shift
                left = jnp.concatenate([tiles[row, t] for t in range(4)], axis=1)
                right = jnp.concatenate([source[ids[row * 4 + t]] for t in range(4)], axis=0)
                value = jnp.dot(left, right, preferred_element_type=F32) * live[row]
                if step > 1:
                    value = 2.0 * value - before[block].astype(F32)
                if step == CHEB:
                    out[out_at + block - DEEP] = value.astype(BF)
                else:
                    target[block] = value.astype(BF)
            return carry

        lax.fori_loop(0, (count - 2 * low) // UNROLL, body, 0)


def inner_kernel(count, ids, live, tiles, vectors, out, even, odd):
    filter_steps(count, 0, ids, live, tiles, vectors, even, odd, out, 0)


def edge_kernel(count, edge, pieces, ids0, live0, ids1, live1, core, tiles, vectors, *refs):
    (vlow, vhigh, tlow_a, tlow_b, thigh_a, thigh_b, out, seg_v, seg_t, even, odd, sems) = refs
    deep_rows = DEEP - REACH
    half = deep_rows // 2
    span = 3 * DEEP
    mine = core[0] * half
    other = half - mine
    copies = []

    def copy(source, target):
        copies.append(pltpu.make_async_copy(source, target, sems.at[len(copies)]))
        copies[-1].start()

    copy(vlow, seg_v.at[0, pl.ds(0, DEEP)])
    copy(vectors.at[pl.ds(0, 2 * DEEP)], seg_v.at[0, pl.ds(DEEP, 2 * DEEP)])
    copy(vectors.at[pl.ds(count - 2 * DEEP, 2 * DEEP)], seg_v.at[1, pl.ds(0, 2 * DEEP)])
    copy(vhigh, seg_v.at[1, pl.ds(2 * DEEP, DEEP)])
    own_rows = 2 * DEEP - REACH
    copy(tlow_a, seg_t.at[0, pl.ds(mine, half)])
    copy(tlow_b, seg_t.at[0, pl.ds(other, half)])
    copy(tiles.at[pl.ds(0, own_rows)], seg_t.at[0, pl.ds(deep_rows, own_rows)])
    copy(tiles.at[pl.ds(count - own_rows, own_rows)], seg_t.at[1, pl.ds(0, own_rows)])
    copy(thigh_a, seg_t.at[1, pl.ds(own_rows + mine, half)])
    copy(thigh_b, seg_t.at[1, pl.ds(own_rows + other, half)])
    for c in copies:
        c.wait()
    filter_steps(span, REACH, ids0, live0, seg_t.at[0], seg_v.at[0], even, odd, out, 0)
    filter_steps(span, REACH, ids1, live1, seg_t.at[1], seg_v.at[1], even, odd, out, DEEP)


def gram_kernel(rows, with_base, quarter, *refs):
    if with_base:
        base, refs = refs[0], refs[1:]
    own, twin, ra, ra2, lb, lb2, oa, oa2, ob, ob2, out, flipped = refs
    q = rows // 4
    for part in range(4):
        flipped[part] = own[pl.ds(part * q, q), :].T

    def add(column, value):
        at = pl.ds(column * 128, 128)
        out[:, at] = value

    def dot(part, piece, at):
        return jnp.dot(flipped[part], piece[pl.ds(at * q, q), :], preferred_element_type=F32)

    i = quarter[0]

    def total(*terms):
        value = terms[0]
        for term in terms[1:]:
            value = value + term
        return value

    values = [
        total(*[dot(p, own, p) for p in range(4)]) * 0.5,
        total(*[dot(p, twin, p) for p in range(4)]) * 0.5,
        dot(0, ra, 0) + dot(1, ra, 1),
        dot(0, ra2, 0) + dot(1, ra2, 1),
        dot(i, oa, 0) + dot(2 + i, ob, 0),
        dot(i, oa2, 0) + dot(2 + i, ob2, 0),
        dot(2, lb, 0) + dot(3, lb, 1),
        dot(2, lb2, 0) + dot(3, lb2, 1),
    ]
    for column, value in enumerate(values):
        if with_base:
            value = value + base[:, column * 128 : (column + 1) * 128]
        add(column, value)


def split(value):
    high = value.astype(BF)
    return high, (value - high.astype(F32)).astype(BF)


def final_kernel(place, scale_in, gathered, *refs):
    pieces, (out, rows_buf, table, matrix, sems) = refs[:36], refs[36:]
    x, y, i = place[0], place[1], place[2]
    low = DEEP * 128
    inner = (rows_buf.shape[0] - 2 * low) // 2
    starts = (
        (low, low + inner, inner // 2),
        (0, low + 2 * inner, low // 2),
    )
    copies = []

    def copy(source, row, count, panel):
        target = rows_buf.at[pl.ds(row, count), pl.ds(panel * 128, 128)]
        copies.append(pltpu.make_async_copy(source, target, sems.at[len(copies)]))
        copies[-1].start()

    def sources():
        for group in range(2):
            yield group, pieces[18 * group : 18 * group + 18]

    for group, refs_of in sources():
        first, second, quarter = starts[group]
        half = 2 * quarter
        for e in range(2):
            if group == 0:
                copy(refs_of[e], first, 2 * half, e)
            else:
                copy(refs_of[e].at[pl.ds(0, half)], first, half, e)
                copy(refs_of[e].at[pl.ds(half, half)], second, half, e)
            ra, rb, la, lb, oa1, oa2, ob1, ob2 = refs_of[2 + 8 * e : 10 + 8 * e]
            copy(ra, first, half, 2 + e)
            copy(rb, second, half, 2 + e)
            copy(la, first, half, 6 + e)
            copy(lb, second, half, 6 + e)
            mine, other = i * quarter, (1 - i) * quarter
            copy(oa1, first + mine, quarter, 4 + e)
            copy(oa2, first + other, quarter, 4 + e)
            copy(ob1, second + mine, quarter, 4 + e)
            copy(ob2, second + other, quarter, 4 + e)

    for dx in range(4):
        for dy in range(4):
            chunk = lax.rem(x + dx, 4) * 4 + lax.rem(y + dy, 4)
            for dz in range(4):
                for e in range(2):
                    piece = gathered[(((e * 4 + dx) * 4 + dy) * 4 + dz)].astype(F32)
                    for qz in range(4):
                        for qe in range(2):
                            column = 2 * ((dz + qz) % 4) + (e ^ qe)
                            table[2 * dz + e, chunk, :, pl.ds(column * 128, 128)] = piece[
                                :, (2 * qz + qe) * 128 : (2 * qz + qe + 1) * 128
                            ]
    width = 1024
    diagonal = lax.broadcasted_iota(jnp.int32, (128, 128), 0) == lax.broadcasted_iota(
        jnp.int32, (128, 128), 1
    )
    eye = diagonal.astype(F32)
    trace = jnp.zeros((128, 128), F32)
    for p in range(8):
        panel = table[p].reshape(128, width)
        matrix[pl.ds(p * 128, 128), :] = panel.astype(BF)
        trace = trace + panel[:, p * 128 : (p + 1) * 128] * eye
    mean = 2.0 * jnp.sum(trace) / float(rows_buf.shape[0] * 16)
    scale = scale_in[0] * mean / width
    kappa = 1.0 / (scale * float(rows_buf.shape[0] * 16))
    own_row = table[0].reshape(128, width)
    own_column = jnp.concatenate(
        [table[p].reshape(128, width)[:, 0:128].T for p in range(8)], axis=1
    )
    unit = jnp.concatenate([eye, jnp.zeros((128, width - 128), F32)], axis=1)
    root = 1.5 * unit - (0.5 * kappa) * (own_row + own_column)

    def times(value):
        both = jnp.concatenate(split(value), axis=0)
        whole = matrix[...]
        product = jnp.dot(both, whole, preferred_element_type=F32) + lax.dot_general(
            both, whole, (((1,), (1,)), ((), ())), preferred_element_type=F32
        )
        return kappa * (product[:128] + product[128:])

    second = 1.5 * root - 0.5 * times(root)
    third = 1.5 * second - 0.5 * times(second)
    result = 1.5 * root - 0.5 * times(third)
    weights = (result / jnp.sqrt(jnp.full((128, width), scale, F32))).astype(BF).T
    for c in copies:
        c.wait()
    step = 512

    def body(turn, carry):
        at = pl.ds(pl.multiple_of(turn * step, step), step)
        out[at, :] = jnp.dot(rows_buf[at, :], weights, preferred_element_type=F32).astype(BF)
        return carry

    lax.fori_loop(0, rows_buf.shape[0] // step, body, 0)


def params(limit):
    return pltpu.CompilerParams(vmem_limit_bytes=limit * 2**20)


def cost(flops, data):
    return pl.CostEstimate(flops=flops, bytes_accessed=data, transcendentals=0)


def local(ham_tiles, tile_columns, stack_lengths, start_vectors, spectral_scale):
    row_count, panel = start_vectors.shape
    blocks = ham_tiles.shape[0]
    total_blocks = blocks * lax.axis_size("row")
    row_at, vec_at = lax.axis_index("row"), lax.axis_index("vec")
    z_at, core_at = vec_at // 2, vec_at % 2
    rows16, zs = lax.axis_size("row"), lax.axis_size("vec") // 2

    def z_perm(move, flip=0):
        return [
            (2 * z + c, 2 * ((z + move) % zs) + (c ^ flip)) for z in range(zs) for c in range(2)
        ]

    def by_z(value, move):
        return lax.ppermute(value, "vec", z_perm(move))

    def swap(value):
        return lax.ppermute(value, "vec", z_perm(0, 1))

    forward = [(r, (r + 1) % rows16) for r in range(rows16)]
    backward = [(r, (r - 1) % rows16) for r in range(rows16)]

    block_ids = row_at * blocks + jnp.arange(blocks, dtype=jnp.int32)
    offsets = (tile_columns - block_ids[:, None] + REACH) % total_blocks - REACH
    local_rows = jnp.arange(blocks, dtype=jnp.int32)
    live = ((local_rows < stack_lengths[0] - REACH) | (local_rows >= blocks - REACH)).astype(
        jnp.int32
    )
    meta = jnp.concatenate([offsets, jnp.broadcast_to(live[:, None], (blocks, 4))], axis=1)
    vectors = start_vectors.reshape(blocks, 128, panel)
    deep_rows = DEEP - REACH
    half = deep_rows // 2
    meta_low = lax.ppermute(meta[blocks - deep_rows :], "row", forward)
    meta_high = lax.ppermute(meta[:deep_rows], "row", backward)
    tiles_low_a = lax.ppermute(
        lax.dynamic_slice_in_dim(ham_tiles, blocks - deep_rows + core_at * half, half, 0),
        "row",
        forward,
    )
    tiles_high_a = lax.ppermute(
        lax.dynamic_slice_in_dim(ham_tiles, core_at * half, half, 0), "row", backward
    )
    vlow = lax.ppermute(vectors[blocks - DEEP :], "row", forward)
    vhigh = lax.ppermute(vectors[:DEEP], "row", backward)
    tiles_low_b = swap(tiles_low_a)
    tiles_high_b = swap(tiles_high_a)

    inner_blocks = blocks - 2 * DEEP
    inner_ids = (local_rows[:, None] + offsets).reshape(-1)
    inner = pl.pallas_call(
        functools.partial(inner_kernel, blocks),
        out_shape=jax.ShapeDtypeStruct((inner_blocks, 128, panel), BF),
        in_specs=[SMEM, SMEM, VMEM, VMEM],
        out_specs=VMEM,
        scratch_shapes=[pltpu.VMEM((blocks, 128, panel), BF)] * 2,
        compiler_params=params(32),
        cost_estimate=cost(10 * 10**9, 11 * 2**20),
        name="inner_filter",
    )(inner_ids, live.astype(F32), ham_tiles, vectors)

    def segment(parts):
        part = jnp.concatenate(parts, axis=0)
        places = REACH + jnp.arange(part.shape[0], dtype=jnp.int32)[:, None] + part[:, :4]
        return places.reshape(-1), part[:, 4].astype(F32)

    own_rows = 2 * DEEP - REACH
    ids0, live0 = segment([meta_low, meta[:own_rows]])
    ids1, live1 = segment([meta[blocks - own_rows :], meta_high])
    inner_flat = inner.reshape(inner_blocks * 128, panel)

    quarter_of = jnp.where(z_at < 2, 0, 1).astype(jnp.int32)
    send_left = jnp.where((z_at + zs - 1) % zs < 2, 0, 1).astype(jnp.int32)
    send_right = jnp.where((z_at + 1) % zs < 2, 0, 1).astype(jnp.int32)

    def needed(own):
        rows = own.shape[0]
        h, q = rows // 2, rows // 4
        twin = swap(own)
        ra = by_z(own[:h], -1)
        lb = by_z(own[h:], 1)
        oa1 = by_z(lax.dynamic_slice_in_dim(ra, send_left * q, q, 0), -1)
        ob1 = by_z(lax.dynamic_slice_in_dim(lb, send_right * q, q, 0), 1)
        return twin, ra, lb, oa1, ob1, swap(ra), swap(lb), swap(oa1), swap(ob1)

    def rest(own, got):
        rows = own.shape[0]
        h, q = rows // 2, rows // 4
        twin, ra, lb, oa1, ob1, ra2, lb2, oa12, ob12 = got
        rb = by_z(own[h:], -1)
        la = by_z(own[:h], 1)
        oa2 = by_z(lax.dynamic_slice_in_dim(ra, (1 - send_left) * q, q, 0), -1)
        ob2 = by_z(lax.dynamic_slice_in_dim(lb, (1 - send_right) * q, q, 0), 1)
        return (
            [own, twin]
            + [ra, rb, la, lb, oa1, oa2, ob1, ob2]
            + [ra2, swap(rb), swap(la), lb2, oa12, swap(oa2), ob12, swap(ob2)]
        )

    def gram(own, got, base):
        twin, ra, lb, oa1, ob1, ra2, lb2, oa12, ob12 = got
        args = [own, twin, ra, ra2, lb, lb2, oa1, oa12, ob1, ob12]
        rows = own.shape[0]
        if base is not None:
            args = [base] + args
        return pl.pallas_call(
            functools.partial(gram_kernel, rows, base is not None),
            out_shape=jax.ShapeDtypeStruct((128, 1024), F32),
            in_specs=[SMEM] + [VMEM] * len(args),
            out_specs=VMEM,
            scratch_shapes=[pltpu.VMEM((4, 128, rows // 4), BF)],
            compiler_params=params(24),
            cost_estimate=cost(rows * 128 * 1024, rows * 128 * 12),
            name="gram",
        )(quarter_of[None], *args)

    inner_got = needed(inner_flat)
    inner_gram = gram(inner_flat, inner_got, None)

    core_arg = core_at.astype(jnp.int32)[None]
    edge = pl.pallas_call(
        functools.partial(edge_kernel, blocks, DEEP, None),
        out_shape=jax.ShapeDtypeStruct((2 * DEEP, 128, panel), BF),
        in_specs=[SMEM] * 5 + [ANY] * 8,
        out_specs=VMEM,
        scratch_shapes=[
            pltpu.VMEM((2, 3 * DEEP, 128, panel), BF),
            pltpu.VMEM((2, 3 * DEEP - 2 * REACH, 4, 128, 128), BF),
            pltpu.VMEM((3 * DEEP, 128, panel), BF),
            pltpu.VMEM((3 * DEEP, 128, panel), BF),
            pltpu.SemaphoreType.DMA((10,)),
        ],
        compiler_params=params(32),
        cost_estimate=cost(8 * 10**9, 11 * 2**20),
        name="edge_filter",
    )(ids0, live0, ids1, live1, core_arg, ham_tiles, vectors, vlow, vhigh,
      tiles_low_a, tiles_low_b, tiles_high_a, tiles_high_b)
    edge_flat = edge.reshape(2 * DEEP * 128, panel)
    edge_got = needed(edge_flat)
    whole_gram = gram(edge_flat, edge_got, inner_gram)

    pieces = lax.all_to_all(
        whole_gram.reshape(rows16, 128 // rows16, 1024), "row", split_axis=0, concat_axis=0
    )
    mine = jnp.sum(pieces, axis=0).astype(BF)[None]

    def around(value, axis, perm_of):
        parts = [value] + [lax.ppermute(value, axis, perm_of(d)) for d in (1, 2, 3)]
        return jnp.concatenate(parts, axis=0)

    def row_perm(dx, dy):
        return [
            (4 * a + b, 4 * ((a - dx) % 4) + (b - dy) % 4) for a in range(4) for b in range(4)
        ]

    got = around(mine, "vec", lambda d: z_perm(-d))
    got = around(got, "row", lambda d: row_perm(0, d))
    got = around(got, "row", lambda d: row_perm(d, 0))
    gathered = jnp.concatenate([got, swap(got)], axis=0)

    inner_all = rest(inner_flat, inner_got)
    edge_all = rest(edge_flat, edge_got)
    place = jnp.stack([row_at // 4, row_at % 4, quarter_of]).astype(jnp.int32)
    return pl.pallas_call(
        final_kernel,
        out_shape=jax.ShapeDtypeStruct((row_count, panel), BF),
        in_specs=[SMEM, SMEM, VMEM] + [ANY] * 36,
        out_specs=VMEM,
        scratch_shapes=[
            pltpu.VMEM((row_count, 1024), BF),
            pltpu.VMEM((8, rows16, 128 // rows16, 1024), F32),
            pltpu.VMEM((1024, 1024), BF),
            pltpu.SemaphoreType.DMA((38,)),
        ],
        compiler_params=params(48),
        cost_estimate=cost(6 * 10**9, 20 * 2**20),
        name="final",
    )(place, spectral_scale, gathered, *inner_all, *edge_all)


def solution(mesh):
    placed = (P("row", None, None, None), P("row", None), P("row"), P("row", "vec"), P())
    return jax.shard_map(
        local, mesh=mesh, in_specs=placed, out_specs=P("row", "vec"), check_vma=False
    )
```

```python
import functools

import jax
import jax.numpy as jnp
from jax import lax
from jax.experimental import pallas as pl
from jax.experimental.pallas import tpu as pltpu
from jax.sharding import PartitionSpec as P

REACH = 2
CHEB = 6
DEEP = REACH * CHEB
BF = jnp.bfloat16
F32 = jnp.float32
ANY = pl.BlockSpec(memory_space=pl.ANY)
SMEM = pl.BlockSpec(memory_space=pltpu.SMEM)
VMEM = pl.BlockSpec(memory_space=pltpu.VMEM)


def filter_steps(count, row_shift, segments, even_odd, out, ready):
    for step in range(1, CHEB + 1):
        low = REACH * step
        turns = 2
        unroll = (count - 2 * low) // turns

        def body(turn, step=step, low=low, unroll=unroll):
            for part in range(unroll):
                for which, (ids, live, tiles, first) in enumerate(segments):
                    even, odd = even_odd[which]
                    source = first if step == 1 else (odd if step % 2 == 0 else even)
                    target = odd if step % 2 else even
                    before = first if step == 2 else target
                    block = low + turn * unroll + part
                    row = block - row_shift
                    left = jnp.concatenate([tiles[row, t] for t in range(4)], axis=1)
                    right = jnp.concatenate([source[ids[row * 4 + t]] for t in range(4)], axis=0)
                    value = jnp.dot(left, right, preferred_element_type=F32) * live[row]
                    if step > 1:
                        value = 2.0 * value - before[block].astype(F32)
                    if step == CHEB:
                        out[which * (count - 2 * low) + turn * unroll + part] = value.astype(BF)
                    else:
                        target[block] = value.astype(BF)

        if step == 1 and ready is not None:
            for turn in range(turns):
                ready(turn)
                body(turn)
        else:

            def looped(turn, carry, body=body):
                body(turn)
                return carry

            lax.fori_loop(0, turns, looped, 0)


def inner_kernel(count, ids, live, tiles, vectors, out, seg_t, seg_v, even, odd, sems):
    half = count // 2
    copies = [
        pltpu.make_async_copy(vectors, seg_v, sems.at[0]),
        pltpu.make_async_copy(tiles.at[pl.ds(0, half)], seg_t.at[pl.ds(0, half)], sems.at[1]),
        pltpu.make_async_copy(
            tiles.at[pl.ds(half, half)], seg_t.at[pl.ds(half, half)], sems.at[2]
        ),
    ]
    for c in copies:
        c.start()

    def ready(turn):
        if turn == 0:
            copies[0].wait()
        copies[1 + turn].wait()

    filter_steps(count, 0, [(ids, live, seg_t, seg_v)], [(even, odd)], out, ready)


def edge_kernel(count, ids0, live0, ids1, live1, core, tiles, vectors, near, far, vlow, vhigh,
                out, seg_v, seg_t, even, odd, even1, odd1, sems):
    deep_rows = DEEP - REACH
    span = 3 * DEEP
    c = core[0]
    own_rows = 2 * DEEP - REACH
    copies = []

    def copy(source, target):
        copies.append(pltpu.make_async_copy(source, target, sems.at[len(copies)]))
        copies[-1].start()

    moved = deep_rows * 4
    for segment, halo, near_v, far_v, far_t in (
        (0, vlow, 0, DEEP, deep_rows),
        (1, vhigh, 2 * DEEP, 0, 0),
    ):
        own_v = 0 if segment == 0 else count - 2 * DEEP
        own_t = 0 if segment == 0 else count - own_rows
        copy(halo.at[pl.ds(0, DEEP)], seg_v.at[segment, pl.ds(near_v, DEEP)])
        copy(vectors.at[pl.ds(own_v, 2 * DEEP)], seg_v.at[segment, pl.ds(far_v, 2 * DEEP)])
        copy(
            tiles.at[pl.ds(own_t * 4, own_rows * 4)],
            seg_t.at[segment, pl.ds(far_t * 4, own_rows * 4)],
        )
    copy(near, seg_t.at[c, pl.ds(c * (own_rows * 4), moved)])
    copy(far, seg_t.at[1 - c, pl.ds((1 - c) * (own_rows * 4), moved)])
    for c in copies:
        c.wait()

    class Rows:
        def __init__(self, which):
            self.which = which

        def __getitem__(self, at):
            return seg_t[self.which, at[0] * 4 + at[1]]

    filter_steps(
        span,
        REACH,
        [
            (ids0, live0, Rows(0), seg_v.at[0]),
            (ids1, live1, Rows(1), seg_v.at[1]),
        ],
        [(even, odd), (even1, odd1)],
        out,
        None,
    )


def gram_kernel(half, with_base, place, *refs):
    if with_base:
        base, refs = refs[0], refs[1:]
    own_in, twin_in, n1, s1, o1, os1, out, flipped, own, twin, beside, across, sems = refs
    i, c = place[2], place[3]
    copies = []

    def copy(source, target):
        copies.append(pltpu.make_async_copy(source, target, sems.at[len(copies)]))
        copies[-1].start()

    copy(own_in, own)
    copy(twin_in, twin)
    for e in range(2):
        copy(n1.at[e], beside.at[c, e])
        copy(s1.at[1 - e], beside.at[1 - c, e])
        copy(o1.at[e], across.at[c, e])
        copy(os1.at[1 - e], across.at[1 - c, e])
    for copied in copies:
        copied.wait()
    q = half // 2
    for part in range(4):
        flipped[part] = own[part * q : (part + 1) * q, :].T

    def dot(part, piece):
        return jnp.dot(flipped[part], piece, preferred_element_type=F32)

    def all_rows(piece):
        return sum(dot(p, piece[p * q : (p + 1) * q]) for p in range(4)) * 0.5

    values = [all_rows(own), all_rows(twin)]
    for e in range(2):
        values.append(dot(0, beside[0, e, :q]) + dot(1, beside[0, e, q:]))
    for e in range(2):
        values.append(dot(i, across[0, e]) + dot(2 + i, across[1, e]))
    for e in range(2):
        values.append(dot(2, beside[1, e, :q]) + dot(3, beside[1, e, q:]))
    for column, value in enumerate(values):
        if with_base:
            value = value + base[:, column * 128 : (column + 1) * 128]
        out[:, column * 128 : (column + 1) * 128] = value


def split(value):
    high = value.astype(BF)
    return high, (value - high.astype(F32)).astype(BF)


def final_kernel(place, scale_in, gathered, gathered_twin, *refs):
    pieces, (out, rows_buf, table, matrix, sems) = refs[:18], refs[18:]
    x, y, i, c = place[0], place[1], place[2], place[3]
    low = DEEP * 128
    total = rows_buf.shape[1]
    inner = (total - 2 * low) // 2
    copies = [[], []]

    def copy(group, source, row, count, panel):
        copied = pltpu.make_async_copy(
            source, rows_buf.at[panel, pl.ds(row, count)], sems.at[len(copies[0]) + len(copies[1])]
        )
        copied.start()
        copies[group].append(copied)

    o2, os2 = pieces[16:18]
    groups = ((low, low + inner, inner, 0), (0, low + 2 * inner, low, inner))
    for group, (first, second, half, at) in enumerate(groups):
        own, twin, n1, s1, o1, os1, n2, s2 = pieces[8 * group : 8 * group + 8]
        q = half // 2
        step = c * (second - first)
        up, down = first + step, second - step
        for e, piece in enumerate((own, twin)):
            copy(group, piece.at[pl.ds(0, half)], first, half, e)
            copy(group, piece.at[pl.ds(half, half)], second, half, e)
        for e in range(2):
            mine, other = i * q, (1 - i) * q
            copy(group, n1.at[e], up, half, 2 + e + 4 * c)
            copy(group, s1.at[1 - e], down, half, 6 + e - 4 * c)
            copy(group, o1.at[e], up + mine, q, 4 + e)
            copy(group, os1.at[1 - e], down + mine, q, 4 + e)
            copy(group, n2.at[e], down, half, 2 + e + 4 * c)
            copy(group, s2.at[1 - e], up, half, 6 + e - 4 * c)
            copy(group, o2.at[pl.ds(at + e * q, q)], up + other, q, 4 + e)
            copy(group, os2.at[pl.ds(at + (1 - e) * q, q)], down + other, q, 4 + e)

    for dx in range(4):
        for dy in range(4):
            chunk = lax.rem(x + dx, 4) * 4 + lax.rem(y + dy, 4)
            for dz in range(4):
                for e in range(2):
                    piece = (gathered_twin if e else gathered)[(dx * 4 + dy) * 4 + dz].astype(F32)
                    for qz in range(4):
                        for qe in range(2):
                            column = 2 * ((dz + qz) % 4) + (e ^ qe)
                            table[2 * dz + e, chunk, :, pl.ds(column * 128, 128)] = piece[
                                :, (2 * qz + qe) * 128 : (2 * qz + qe + 1) * 128
                            ]
    width = 1024
    diagonal = lax.broadcasted_iota(jnp.int32, (128, 128), 0) == lax.broadcasted_iota(
        jnp.int32, (128, 128), 1
    )
    eye = diagonal.astype(F32)
    trace = jnp.zeros((128, 128), F32)
    for p in range(8):
        panel = table[p].reshape(128, width)
        matrix[pl.ds(p * 128, 128), :] = panel.astype(BF)
        trace = trace + panel[:, p * 128 : (p + 1) * 128] * eye
    mean = 2.0 * jnp.sum(trace) / float(total * 16)
    scale = scale_in[0] * mean / width
    kappa = 1.0 / (scale * float(total * 16))
    own_row = table[0].reshape(128, width)
    own_column = jnp.concatenate(
        [table[p].reshape(128, width)[:, 0:128].T for p in range(8)], axis=1
    )
    unit = jnp.concatenate([eye, jnp.zeros((128, width - 128), F32)], axis=1)
    root = 1.5 * unit - (0.5 * kappa) * (own_row + own_column)

    def times(value):
        both = jnp.concatenate(split(value), axis=0)
        whole = matrix[...]
        product = jnp.dot(both, whole, preferred_element_type=F32) + lax.dot_general(
            both, whole, (((1,), (1,)), ((), ())), preferred_element_type=F32
        )
        return kappa * (product[:128] + product[128:])

    second = 1.5 * root - 0.5 * times(root)
    third = 1.5 * second - 0.5 * times(second)
    result = 1.5 * root - 0.5 * times(third)
    weights = (result / jnp.sqrt(jnp.full((128, width), scale, F32))).astype(BF).T
    step = 512
    ranges = ([(low, low + 2 * inner)], [(0, low), (low + 2 * inner, total)])
    for group in range(2):
        for copied in copies[group]:
            copied.wait()
        for begin, end in ranges[group]:
            for row in range(begin, end, step):
                left = jnp.concatenate([rows_buf[p, row : row + step] for p in range(8)], axis=1)
                product = jnp.dot(left, weights, preferred_element_type=F32)
                out[row : row + step] = product.astype(BF)


def params(limit):
    return pltpu.CompilerParams(vmem_limit_bytes=limit * 2**20)


def cost(flops, data):
    return pl.CostEstimate(flops=flops, bytes_accessed=data, transcendentals=0)


def local(ham_tiles, tile_columns, stack_lengths, start_vectors, spectral_scale):
    row_count, panel = start_vectors.shape
    blocks = ham_tiles.shape[0]
    total_blocks = blocks * lax.axis_size("row")
    row_at, vec_at = lax.axis_index("row"), lax.axis_index("vec")
    z_at, core_at = vec_at // 2, vec_at % 2
    rows16, zs = lax.axis_size("row"), lax.axis_size("vec") // 2

    def z_perm(move, flip=0):
        return [
            (2 * z + c, 2 * ((z + move) % zs) + (c ^ flip)) for z in range(zs) for c in range(2)
        ]

    def by_z(value, move):
        return lax.ppermute(value, "vec", z_perm(move))

    def swap(value):
        return lax.ppermute(value, "vec", z_perm(0, 1))

    forward = [(r, (r + 1) % rows16) for r in range(rows16)]
    backward = [(r, (r - 1) % rows16) for r in range(rows16)]

    block_ids = row_at * blocks + jnp.arange(blocks, dtype=jnp.int32)
    offsets = (tile_columns - block_ids[:, None] + REACH) % total_blocks - REACH
    local_rows = jnp.arange(blocks, dtype=jnp.int32)
    live = ((local_rows < stack_lengths[0] - REACH) | (local_rows >= blocks - REACH)).astype(
        jnp.int32
    )
    meta = jnp.concatenate([offsets, jnp.broadcast_to(live[:, None], (blocks, 4))], axis=1)
    vectors = start_vectors.reshape(blocks, 128, panel)
    flat_tiles = ham_tiles.reshape(blocks * 4, 128, 128)
    deep_rows = DEEP - REACH

    devices = [(r, z, c) for r in range(rows16) for z in range(zs) for c in range(2)]
    row_sides = [
        ((r * zs + z) * 2 + c, ((r + 1 - 2 * c) % rows16 * zs + z) * 2 + c) for r, z, c in devices
    ]
    sides = [(2 * z + c, 2 * ((z - 1 + 2 * c) % zs) + c) for z in range(zs) for c in range(2)]

    def with_facts(part, facts):
        block = jnp.pad(facts.astype(BF), ((0, 128 - deep_rows), (0, 120)))[None]
        return jnp.concatenate([part, block], axis=0)

    near = lax.ppermute(
        lax.dynamic_slice_in_dim(
            flat_tiles, (1 - core_at) * (4 * (blocks - deep_rows)), 4 * deep_rows, 0
        ),
        ("row", "vec"),
        row_sides,
    )
    vlow = lax.ppermute(
        with_facts(vectors[blocks - DEEP :], meta[blocks - deep_rows :]), "row", forward
    )
    vhigh = lax.ppermute(with_facts(vectors[:DEEP], meta[:deep_rows]), "row", backward)
    near, vlow, vhigh = lax.optimization_barrier((near, vlow, vhigh))
    far = swap(near)
    meta_low = vlow[-1, :deep_rows, :8].astype(jnp.int32)
    meta_high = vhigh[-1, :deep_rows, :8].astype(jnp.int32)

    inner_blocks = blocks - 2 * DEEP
    inner_ids = (local_rows[:, None] + offsets).reshape(-1)
    inner = pl.pallas_call(
        functools.partial(inner_kernel, blocks),
        out_shape=jax.ShapeDtypeStruct((inner_blocks, 128, panel), BF),
        in_specs=[SMEM, SMEM, ANY, ANY],
        out_specs=VMEM,
        scratch_shapes=[
            pltpu.VMEM((blocks, 4, 128, 128), BF),
            pltpu.VMEM((blocks, 128, panel), BF),
            pltpu.VMEM((blocks, 128, panel), BF),
            pltpu.VMEM((blocks, 128, panel), BF),
            pltpu.SemaphoreType.DMA((3,)),
        ],
        compiler_params=params(58),
        cost_estimate=cost(10**6, 2**20),
        name="inner_filter",
    )(inner_ids, live.astype(F32), ham_tiles, vectors)

    def segment(parts):
        part = jnp.concatenate(parts, axis=0)
        places = REACH + jnp.arange(part.shape[0], dtype=jnp.int32)[:, None] + part[:, :4]
        return places.reshape(-1), part[:, 4].astype(F32)

    own_rows = 2 * DEEP - REACH
    ids0, live0 = segment([meta_low, meta[:own_rows]])
    ids1, live1 = segment([meta[blocks - own_rows :], meta_high])
    inner_own = inner.reshape(inner_blocks * 128, panel)

    quarter_of = jnp.where(z_at < 2, 0, 1).astype(jnp.int32)
    send_left = jnp.where((z_at + zs - 1) % zs < 2, 0, 1).astype(jnp.int32)
    send_right = jnp.where((z_at + 1) % zs < 2, 0, 1).astype(jnp.int32)

    place = jnp.stack([row_at // 4, row_at % 4, quarter_of, core_at]).astype(jnp.int32)
    forward_part = jnp.where(core_at == 0, send_left, send_right)

    def half_of(value, which):
        h = value.shape[0] // 2
        return lax.dynamic_slice_in_dim(value, which * h, h, 0)

    def pieces_of(pair_value, which):
        h = pair_value.shape[0] // 2
        q = h // 2
        return [lax.dynamic_slice_in_dim(pair_value, e * h + which * q, q, 0) for e in range(2)]

    def join(parts):
        return jnp.concatenate(parts, axis=0)

    def by_side(value):
        return lax.ppermute(value, "vec", sides)

    def needed(own, before_send, before_forward):
        twin = swap(own)
        sent, *_ = lax.optimization_barrier(
            (join([half_of(own, core_at), half_of(twin, core_at)]), *before_send)
        )
        n1 = by_side(sent)
        n1_late, *_ = lax.optimization_barrier((n1, *before_forward))
        o1 = by_side(join(pieces_of(n1_late, forward_part)))
        return own, twin, n1, swap(n1), o1, swap(o1)

    def rest_of(own, twin):
        return join([half_of(own, 1 - core_at), half_of(twin, 1 - core_at)])

    def two(value):
        return value.reshape(2, value.shape[0] // 2, panel)

    def gram(got, base):
        args = list(got[:2]) + [two(v) for v in got[2:]]
        half = got[0].shape[0] // 2
        return pl.pallas_call(
            functools.partial(gram_kernel, half, base is not None),
            out_shape=jax.ShapeDtypeStruct((128, 1024), F32),
            in_specs=[SMEM] + [VMEM] * (base is not None) + [ANY] * len(args),
            out_specs=VMEM,
            scratch_shapes=[
                pltpu.VMEM((4, 128, half // 2), BF),
                pltpu.VMEM((2 * half, panel), BF),
                pltpu.VMEM((2 * half, panel), BF),
                pltpu.VMEM((2, 2, half, panel), BF),
                pltpu.VMEM((2, 2, half // 2, panel), BF),
                pltpu.SemaphoreType.DMA((10,)),
            ],
            compiler_params=params(56),
            cost_estimate=cost(half * 256 * 1024, half * 128 * 24),
            name="gram",
        )(place, *([base] if base is not None else []), *args)

    inner_got = needed(inner_own, (far, vlow, vhigh), ())
    inner_gram = gram(inner_got, None)
    inner_rest, _ = lax.optimization_barrier((rest_of(*inner_got[:2]), inner_got[4]))
    inner_n2 = by_side(inner_rest)
    core_arg = core_at.astype(jnp.int32)[None]
    edge = pl.pallas_call(
        functools.partial(edge_kernel, blocks),
        out_shape=jax.ShapeDtypeStruct((2 * DEEP, 128, panel), BF),
        in_specs=[SMEM] * 5 + [ANY] * 6,
        out_specs=VMEM,
        scratch_shapes=[
            pltpu.VMEM((2, 3 * DEEP, 128, panel), BF),
            pltpu.VMEM((2, (3 * DEEP - 2 * REACH) * 4, 128, 128), BF),
        ]
        + [pltpu.VMEM((3 * DEEP, 128, panel), BF)] * 4
        + [pltpu.SemaphoreType.DMA((10,))],
        compiler_params=params(58),
        cost_estimate=cost(8 * 10**9, 11 * 2**20),
        name="edge_filter",
    )(ids0, live0, ids1, live1, core_arg, flat_tiles, vectors, near, far, vlow, vhigh)
    edge_own = edge.reshape(2 * DEEP * 128, panel)
    edge_got = needed(edge_own, (), (inner_gram, inner_n2))
    whole_gram = gram(edge_got, inner_gram)

    pieces = lax.all_to_all(
        whole_gram.reshape(rows16, 128 // rows16, 1024), "row", split_axis=0, concat_axis=0
    )
    mine = jnp.sum(pieces, axis=0).astype(BF)[None]

    def around(value, axis, perm_of):
        parts = [value] + [lax.ppermute(value, axis, perm_of(d)) for d in (1, 2, 3)]
        return jnp.concatenate(parts, axis=0)

    def row_perm(dx, dy):
        return [
            (4 * a + b, 4 * ((a - dx) % 4) + (b - dy) % 4) for a in range(4) for b in range(4)
        ]

    got = around(mine, "vec", lambda d: z_perm(-d))
    later = lax.optimization_barrier(
        (
            rest_of(*edge_got[:2]),
            join(pieces_of(inner_got[2], 1 - forward_part) + pieces_of(edge_got[2], 1 - forward_part)),
            got,
        )
    )
    edge_n2, o2 = by_side(later[0]), by_side(later[1])
    got = around(got, "row", lambda d: row_perm(0, d))
    got = around(got, "row", lambda d: row_perm(d, 0))
    parts = []
    for values, n2 in ((inner_got, inner_n2), (edge_got, edge_n2)):
        parts += list(values[:2]) + [two(v) for v in (*values[2:], n2, swap(n2))]
    parts += [o2, swap(o2)]
    return pl.pallas_call(
        final_kernel,
        out_shape=jax.ShapeDtypeStruct((row_count, panel), BF),
        in_specs=[SMEM, SMEM, VMEM, VMEM] + [ANY] * len(parts),
        out_specs=VMEM,
        scratch_shapes=[
            pltpu.VMEM((8, row_count, 128), BF),
            pltpu.VMEM((8, rows16, 128 // rows16, 1024), F32),
            pltpu.VMEM((1024, 1024), BF),
            pltpu.SemaphoreType.DMA((40,)),
        ],
        compiler_params=params(58),
        cost_estimate=cost(6 * 10**9, 20 * 2**20),
        name="final",
    )(place, spectral_scale, got, swap(got), *parts)


def solution(mesh):
    placed = (P("row", None, None, None), P("row", None), P("row"), P("row", "vec"), P())
    return jax.shard_map(
        local, mesh=mesh, in_specs=placed, out_specs=P("row", "vec"), check_vma=False
    )
```

```python
import functools

import jax
import jax.numpy as jnp
from jax import lax
from jax.experimental import pallas as pl
from jax.experimental.pallas import tpu as pltpu
from jax.sharding import PartitionSpec as P

REACH = 2
CHEB = 6
DEEP = REACH * CHEB
BF = jnp.bfloat16
F32 = jnp.float32
ANY = pl.BlockSpec(memory_space=pl.ANY)
SMEM = pl.BlockSpec(memory_space=pltpu.SMEM)
VMEM = pl.BlockSpec(memory_space=pltpu.VMEM)


def filter_steps(count, row_shift, segments, even_odd, out, ready):
    for step in range(1, CHEB + 1):
        low = REACH * step
        turns = 2
        unroll = (count - 2 * low) // turns

        def body(turn, step=step, low=low, unroll=unroll):
            for part in range(unroll):
                for which, (ids, live, tiles, first) in enumerate(segments):
                    even, odd = even_odd[which]
                    source = first if step == 1 else (odd if step % 2 == 0 else even)
                    target = odd if step % 2 else even
                    before = first if step == 2 else target
                    block = low + turn * unroll + part
                    row = block - row_shift
                    left = jnp.concatenate([tiles[row, t] for t in range(4)], axis=1)
                    right = jnp.concatenate([source[ids[row * 4 + t]] for t in range(4)], axis=0)
                    value = jnp.dot(left, right, preferred_element_type=F32) * live[row]
                    if step > 1:
                        value = 2.0 * value - before[block].astype(F32)
                    if step == CHEB:
                        out[which * (count - 2 * low) + turn * unroll + part] = value.astype(BF)
                    else:
                        target[block] = value.astype(BF)

        if step == 1 and ready is not None:
            for turn in range(turns):
                ready(turn)
                body(turn)
        else:

            def looped(turn, carry, body=body):
                body(turn)
                return carry

            lax.fori_loop(0, turns, looped, 0)


def inner_kernel(count, ids, live, tiles, vectors, out, seg_t, seg_v, even, odd, sems):
    half = count // 2
    copies = [
        pltpu.make_async_copy(vectors, seg_v, sems.at[0]),
        pltpu.make_async_copy(tiles.at[pl.ds(0, half)], seg_t.at[pl.ds(0, half)], sems.at[1]),
        pltpu.make_async_copy(
            tiles.at[pl.ds(half, half)], seg_t.at[pl.ds(half, half)], sems.at[2]
        ),
    ]
    for c in copies:
        c.start()

    def ready(turn):
        if turn == 0:
            copies[0].wait()
        copies[1 + turn].wait()

    filter_steps(count, 0, [(ids, live, seg_t, seg_v)], [(even, odd)], out, ready)


def edge_kernel(count, ids0, live0, ids1, live1, core, tiles, vectors, near, far, vlow, vhigh,
                out, seg_v, seg_t, even, odd, even1, odd1, sems):
    deep_rows = DEEP - REACH
    span = 3 * DEEP
    c = core[0]
    own_rows = 2 * DEEP - REACH
    copies = []

    def copy(source, target):
        copies.append(pltpu.make_async_copy(source, target, sems.at[len(copies)]))
        copies[-1].start()

    moved = deep_rows * 4
    for segment, halo, near_v, far_v, far_t in (
        (0, vlow, 0, DEEP, deep_rows),
        (1, vhigh, 2 * DEEP, 0, 0),
    ):
        own_v = 0 if segment == 0 else count - 2 * DEEP
        own_t = 0 if segment == 0 else count - own_rows
        copy(halo.at[pl.ds(0, DEEP)], seg_v.at[segment, pl.ds(near_v, DEEP)])
        copy(vectors.at[pl.ds(own_v, 2 * DEEP)], seg_v.at[segment, pl.ds(far_v, 2 * DEEP)])
        copy(
            tiles.at[pl.ds(own_t * 4, own_rows * 4)],
            seg_t.at[segment, pl.ds(far_t * 4, own_rows * 4)],
        )
    copy(near, seg_t.at[c, pl.ds(c * (own_rows * 4), moved)])
    copy(far, seg_t.at[1 - c, pl.ds((1 - c) * (own_rows * 4), moved)])
    for c in copies:
        c.wait()

    class Rows:
        def __init__(self, which):
            self.which = which

        def __getitem__(self, at):
            return seg_t[self.which, at[0] * 4 + at[1]]

    filter_steps(
        span,
        REACH,
        [
            (ids0, live0, Rows(0), seg_v.at[0]),
            (ids1, live1, Rows(1), seg_v.at[1]),
        ],
        [(even, odd), (even1, odd1)],
        out,
        None,
    )


def gram_kernel(half, with_base, place, *refs):
    if with_base:
        base, refs = refs[0], refs[1:]
    own_in, twin_in, n1, s1, o1, os1, out, flipped, own, twin, beside, across, sems = refs
    i, c = place[2], place[3]
    copies = []

    def copy(source, target):
        copies.append(pltpu.make_async_copy(source, target, sems.at[len(copies)]))
        copies[-1].start()

    copy(own_in, own)
    copy(twin_in, twin)
    for e in range(2):
        copy(n1.at[e], beside.at[c, e])
        copy(s1.at[1 - e], beside.at[1 - c, e])
        copy(o1.at[e], across.at[c, e])
        copy(os1.at[1 - e], across.at[1 - c, e])
    for copied in copies:
        copied.wait()
    q = half // 2
    for part in range(4):
        flipped[part] = own[part * q : (part + 1) * q, :].T

    def dot(part, piece):
        return jnp.dot(flipped[part], piece, preferred_element_type=F32)

    def all_rows(piece):
        return sum(dot(p, piece[p * q : (p + 1) * q]) for p in range(4)) * 0.5

    values = [all_rows(own), all_rows(twin)]
    for e in range(2):
        values.append(dot(0, beside[0, e, :q]) + dot(1, beside[0, e, q:]))
    for e in range(2):
        values.append(dot(i, across[0, e]) + dot(2 + i, across[1, e]))
    for e in range(2):
        values.append(dot(2, beside[1, e, :q]) + dot(3, beside[1, e, q:]))
    for column, value in enumerate(values):
        if with_base:
            value = value + base[:, column * 128 : (column + 1) * 128]
        out[:, column * 128 : (column + 1) * 128] = value


def split(value):
    high = value.astype(BF)
    return high, (value - high.astype(F32)).astype(BF)


def final_kernel(place, scale_in, gathered, gathered_twin, *refs):
    pieces, (out, rows_buf, table, matrix, sems) = refs[:16], refs[16:]
    x, y, i, c = place[0], place[1], place[2], place[3]
    low = DEEP * 128
    total = rows_buf.shape[1]
    inner = (total - 2 * low) // 2
    copies = [[], []]

    def copy(group, source, row, count, panel):
        copied = pltpu.make_async_copy(
            source, rows_buf.at[panel, pl.ds(row, count)], sems.at[len(copies[0]) + len(copies[1])]
        )
        copied.start()
        copies[group].append(copied)

    n2, s2, o2, os2 = pieces[12:16]
    groups = ((low, low + inner, inner, 0), (0, low + 2 * inner, low, inner))
    for group, (first, second, half, at) in enumerate(groups):
        own, twin, n1, s1, o1, os1 = pieces[6 * group : 6 * group + 6]
        q = half // 2
        step = c * (second - first)
        up, down = first + step, second - step
        for e, piece in enumerate((own, twin)):
            copy(group, piece.at[pl.ds(0, half)], first, half, e)
            copy(group, piece.at[pl.ds(half, half)], second, half, e)
        for e in range(2):
            mine, other = i * q, (1 - i) * q
            copy(group, n1.at[e], up, half, 2 + e + 4 * c)
            copy(group, s1.at[1 - e], down, half, 6 + e - 4 * c)
            copy(group, o1.at[e], up + mine, q, 4 + e)
            copy(group, os1.at[1 - e], down + mine, q, 4 + e)
            copy(group, n2.at[pl.ds(2 * at + e * half, half)], down, half, 2 + e + 4 * c)
            copy(group, s2.at[pl.ds(2 * at + (1 - e) * half, half)], up, half, 6 + e - 4 * c)
            copy(group, o2.at[pl.ds(at + e * q, q)], up + other, q, 4 + e)
            copy(group, os2.at[pl.ds(at + (1 - e) * q, q)], down + other, q, 4 + e)

    for dx in range(4):
        for dy in range(4):
            chunk = lax.rem(x + dx, 4) * 4 + lax.rem(y + dy, 4)
            for dz in range(4):
                for e in range(2):
                    piece = (gathered_twin if e else gathered)[(dx * 4 + dy) * 4 + dz].astype(F32)
                    for qz in range(4):
                        for qe in range(2):
                            column = 2 * ((dz + qz) % 4) + (e ^ qe)
                            table[2 * dz + e, chunk, :, pl.ds(column * 128, 128)] = piece[
                                :, (2 * qz + qe) * 128 : (2 * qz + qe + 1) * 128
                            ]
    width = 1024
    diagonal = lax.broadcasted_iota(jnp.int32, (128, 128), 0) == lax.broadcasted_iota(
        jnp.int32, (128, 128), 1
    )
    eye = diagonal.astype(F32)
    trace = jnp.zeros((128, 128), F32)
    for p in range(8):
        panel = table[p].reshape(128, width)
        matrix[pl.ds(p * 128, 128), :] = panel.astype(BF)
        trace = trace + panel[:, p * 128 : (p + 1) * 128] * eye
    mean = 2.0 * jnp.sum(trace) / float(total * 16)
    scale = scale_in[0] * mean / width
    kappa = 1.0 / (scale * float(total * 16))
    own_row = table[0].reshape(128, width)
    own_column = jnp.concatenate(
        [table[p].reshape(128, width)[:, 0:128].T for p in range(8)], axis=1
    )
    unit = jnp.concatenate([eye, jnp.zeros((128, width - 128), F32)], axis=1)
    root = 1.5 * unit - (0.5 * kappa) * (own_row + own_column)

    def times(value):
        both = jnp.concatenate(split(value), axis=0)
        whole = matrix[...]
        product = jnp.dot(both, whole, preferred_element_type=F32) + lax.dot_general(
            both, whole, (((1,), (1,)), ((), ())), preferred_element_type=F32
        )
        return kappa * (product[:128] + product[128:])

    second = 1.5 * root - 0.5 * times(root)
    third = 1.5 * second - 0.5 * times(second)
    result = 1.5 * root - 0.5 * times(third)
    weights = (result / jnp.sqrt(jnp.full((128, width), scale, F32))).astype(BF).T
    step = 512
    ranges = ([(low, low + 2 * inner)], [(0, low), (low + 2 * inner, total)])
    for group in range(2):
        for copied in copies[group]:
            copied.wait()
        for begin, end in ranges[group]:
            for row in range(begin, end, step):
                left = jnp.concatenate([rows_buf[p, row : row + step] for p in range(8)], axis=1)
                product = jnp.dot(left, weights, preferred_element_type=F32)
                out[row : row + step] = product.astype(BF)


def params(limit):
    return pltpu.CompilerParams(vmem_limit_bytes=limit * 2**20)


def cost(flops, data):
    return pl.CostEstimate(flops=flops, bytes_accessed=data, transcendentals=0)


def local(ham_tiles, tile_columns, stack_lengths, start_vectors, spectral_scale):
    row_count, panel = start_vectors.shape
    blocks = ham_tiles.shape[0]
    total_blocks = blocks * lax.axis_size("row")
    row_at, vec_at = lax.axis_index("row"), lax.axis_index("vec")
    z_at, core_at = vec_at // 2, vec_at % 2
    rows16, zs = lax.axis_size("row"), lax.axis_size("vec") // 2

    def z_perm(move, flip=0):
        return [
            (2 * z + c, 2 * ((z + move) % zs) + (c ^ flip)) for z in range(zs) for c in range(2)
        ]

    def by_z(value, move):
        return lax.ppermute(value, "vec", z_perm(move))

    def swap(value):
        return lax.ppermute(value, "vec", z_perm(0, 1))

    forward = [(r, (r + 1) % rows16) for r in range(rows16)]
    backward = [(r, (r - 1) % rows16) for r in range(rows16)]

    block_ids = row_at * blocks + jnp.arange(blocks, dtype=jnp.int32)
    offsets = (tile_columns - block_ids[:, None] + REACH) % total_blocks - REACH
    local_rows = jnp.arange(blocks, dtype=jnp.int32)
    live = ((local_rows < stack_lengths[0] - REACH) | (local_rows >= blocks - REACH)).astype(
        jnp.int32
    )
    meta = jnp.concatenate([offsets, jnp.broadcast_to(live[:, None], (blocks, 4))], axis=1)
    vectors = start_vectors.reshape(blocks, 128, panel)
    flat_tiles = ham_tiles.reshape(blocks * 4, 128, 128)
    deep_rows = DEEP - REACH

    devices = [(r, z, c) for r in range(rows16) for z in range(zs) for c in range(2)]
    row_sides = [
        ((r * zs + z) * 2 + c, ((r + 1 - 2 * c) % rows16 * zs + z) * 2 + c) for r, z, c in devices
    ]
    sides = [(2 * z + c, 2 * ((z - 1 + 2 * c) % zs) + c) for z in range(zs) for c in range(2)]

    def with_facts(part, facts):
        block = jnp.pad(facts.astype(BF), ((0, 128 - deep_rows), (0, 120)))[None]
        return jnp.concatenate([part, block], axis=0)

    near = lax.ppermute(
        lax.dynamic_slice_in_dim(
            flat_tiles, (1 - core_at) * (4 * (blocks - deep_rows)), 4 * deep_rows, 0
        ),
        ("row", "vec"),
        row_sides,
    )
    vlow = lax.ppermute(
        with_facts(vectors[blocks - DEEP :], meta[blocks - deep_rows :]), "row", forward
    )
    vhigh = lax.ppermute(with_facts(vectors[:DEEP], meta[:deep_rows]), "row", backward)
    near, vlow, vhigh = lax.optimization_barrier((near, vlow, vhigh))
    far = swap(near)
    meta_low = vlow[-1, :deep_rows, :8].astype(jnp.int32)
    meta_high = vhigh[-1, :deep_rows, :8].astype(jnp.int32)

    inner_blocks = blocks - 2 * DEEP
    inner_ids = (local_rows[:, None] + offsets).reshape(-1)
    inner = pl.pallas_call(
        functools.partial(inner_kernel, blocks),
        out_shape=jax.ShapeDtypeStruct((inner_blocks, 128, panel), BF),
        in_specs=[SMEM, SMEM, ANY, ANY],
        out_specs=VMEM,
        scratch_shapes=[
            pltpu.VMEM((blocks, 4, 128, 128), BF),
            pltpu.VMEM((blocks, 128, panel), BF),
            pltpu.VMEM((blocks, 128, panel), BF),
            pltpu.VMEM((blocks, 128, panel), BF),
            pltpu.SemaphoreType.DMA((3,)),
        ],
        compiler_params=params(58),
        cost_estimate=cost(10**6, 2**20),
        name="inner_filter",
    )(inner_ids, live.astype(F32), ham_tiles, vectors)

    def segment(parts):
        part = jnp.concatenate(parts, axis=0)
        places = REACH + jnp.arange(part.shape[0], dtype=jnp.int32)[:, None] + part[:, :4]
        return places.reshape(-1), part[:, 4].astype(F32)

    own_rows = 2 * DEEP - REACH
    ids0, live0 = segment([meta_low, meta[:own_rows]])
    ids1, live1 = segment([meta[blocks - own_rows :], meta_high])
    inner_own = inner.reshape(inner_blocks * 128, panel)

    quarter_of = jnp.where(z_at < 2, 0, 1).astype(jnp.int32)
    send_left = jnp.where((z_at + zs - 1) % zs < 2, 0, 1).astype(jnp.int32)
    send_right = jnp.where((z_at + 1) % zs < 2, 0, 1).astype(jnp.int32)

    place = jnp.stack([row_at // 4, row_at % 4, quarter_of, core_at]).astype(jnp.int32)
    forward_part = jnp.where(core_at == 0, send_left, send_right)

    def half_of(value, which):
        h = value.shape[0] // 2
        return lax.dynamic_slice_in_dim(value, which * h, h, 0)

    def pieces_of(pair_value, which):
        h = pair_value.shape[0] // 2
        q = h // 2
        return [lax.dynamic_slice_in_dim(pair_value, e * h + which * q, q, 0) for e in range(2)]

    def join(parts):
        return jnp.concatenate(parts, axis=0)

    def by_side(value):
        return lax.ppermute(value, "vec", sides)

    def send_near(own, before):
        twin = swap(own)
        sent, *_ = lax.optimization_barrier(
            (join([half_of(own, core_at), half_of(twin, core_at)]), *before)
        )
        return own, twin, sent, by_side(sent)

    def rest_of(own, twin):
        return join([half_of(own, 1 - core_at), half_of(twin, 1 - core_at)])

    def two(value):
        return value.reshape(2, value.shape[0] // 2, panel)

    def gram(got, base):
        args = list(got[:2]) + [two(v) for v in got[2:]]
        half = got[0].shape[0] // 2
        return pl.pallas_call(
            functools.partial(gram_kernel, half, base is not None),
            out_shape=jax.ShapeDtypeStruct((128, 1024), F32),
            in_specs=[SMEM] + [VMEM] * (base is not None) + [ANY] * len(args),
            out_specs=VMEM,
            scratch_shapes=[
                pltpu.VMEM((4, 128, half // 2), BF),
                pltpu.VMEM((2 * half, panel), BF),
                pltpu.VMEM((2 * half, panel), BF),
                pltpu.VMEM((2, 2, half, panel), BF),
                pltpu.VMEM((2, 2, half // 2, panel), BF),
                pltpu.SemaphoreType.DMA((10,)),
            ],
            compiler_params=params(56),
            cost_estimate=cost(half * 256 * 1024, half * 128 * 24),
            name="gram",
        )(place, *([base] if base is not None else []), *args)

    own, twin, _, n1 = send_near(inner_own, (far, vlow, vhigh))
    inner_near = [own, twin, n1, swap(n1), by_side(join(pieces_of(n1, forward_part)))]
    core_arg = core_at.astype(jnp.int32)[None]
    edge = pl.pallas_call(
        functools.partial(edge_kernel, blocks),
        out_shape=jax.ShapeDtypeStruct((2 * DEEP, 128, panel), BF),
        in_specs=[SMEM] * 5 + [ANY] * 6,
        out_specs=VMEM,
        scratch_shapes=[
            pltpu.VMEM((2, 3 * DEEP, 128, panel), BF),
            pltpu.VMEM((2, (3 * DEEP - 2 * REACH) * 4, 128, 128), BF),
        ]
        + [pltpu.VMEM((3 * DEEP, 128, panel), BF)] * 4
        + [pltpu.SemaphoreType.DMA((10,))],
        compiler_params=params(58),
        cost_estimate=cost(8 * 10**9, 11 * 2**20),
        name="edge_filter",
    )(ids0, live0, ids1, live1, core_arg, flat_tiles, vectors, near, far, vlow, vhigh)
    edge_own = edge.reshape(2 * DEEP * 128, panel)
    own, twin, sent, n1 = send_near(edge_own, ())
    o1, _ = lax.optimization_barrier((inner_near[4], sent))
    inner_got = inner_near[:4] + [o1, swap(o1)]
    inner_gram = gram(inner_got, None)
    n1_late, _ = lax.optimization_barrier((n1, inner_gram))
    o1 = by_side(join(pieces_of(n1_late, forward_part)))
    edge_got = [own, twin, n1, swap(n1), o1, swap(o1)]
    whole_gram = gram(edge_got, inner_gram)

    late, _ = lax.optimization_barrier(
        (join([rest_of(*inner_got[:2]), rest_of(*edge_got[:2])]), o1)
    )
    n2 = by_side(late)

    pieces = lax.all_to_all(
        whole_gram.reshape(rows16, 128 // rows16, 1024), "row", split_axis=0, concat_axis=0
    )
    mine = jnp.sum(pieces, axis=0).astype(BF)[None]
    mine, n2 = lax.optimization_barrier((mine, n2))

    def around(value, axis, perm_of):
        parts = [value] + [lax.ppermute(value, axis, perm_of(d)) for d in (1, 2, 3)]
        return jnp.concatenate(parts, axis=0)

    def row_perm(dx, dy):
        return [
            (4 * a + b, 4 * ((a - dx) % 4) + (b - dy) % 4) for a in range(4) for b in range(4)
        ]

    got = around(mine, "vec", lambda d: z_perm(-d))
    later, _ = lax.optimization_barrier(
        (
            join(pieces_of(inner_got[2], 1 - forward_part) + pieces_of(edge_got[2], 1 - forward_part)),
            got,
        )
    )
    o2 = by_side(later)
    got = around(got, "row", lambda d: row_perm(0, d))
    got = around(got, "row", lambda d: row_perm(d, 0))
    parts = []
    for values in (inner_got, edge_got):
        parts += list(values[:2]) + [two(v) for v in values[2:]]
    parts += [n2, swap(n2), o2, swap(o2)]
    return pl.pallas_call(
        final_kernel,
        out_shape=jax.ShapeDtypeStruct((row_count, panel), BF),
        in_specs=[SMEM, SMEM, VMEM, VMEM] + [ANY] * len(parts),
        out_specs=VMEM,
        scratch_shapes=[
            pltpu.VMEM((8, row_count, 128), BF),
            pltpu.VMEM((8, rows16, 128 // rows16, 1024), F32),
            pltpu.VMEM((1024, 1024), BF),
            pltpu.SemaphoreType.DMA((40,)),
        ],
        compiler_params=params(58),
        cost_estimate=cost(6 * 10**9, 20 * 2**20),
        name="final",
    )(place, spectral_scale, got, swap(got), *parts)


def solution(mesh):
    placed = (P("row", None, None, None), P("row", None), P("row"), P("row", "vec"), P())
    return jax.shard_map(
        local, mesh=mesh, in_specs=placed, out_specs=P("row", "vec"), check_vma=False
    )
```

```python
import functools

import jax
import jax.numpy as jnp
from jax import lax
from jax.experimental import pallas as pl
from jax.experimental.pallas import tpu as pltpu
from jax.sharding import PartitionSpec as P

REACH = 2
CHEB = 6
DEEP = REACH * CHEB
BF = jnp.bfloat16
F32 = jnp.float32
ANY = pl.BlockSpec(memory_space=pl.ANY)
SMEM = pl.BlockSpec(memory_space=pltpu.SMEM)
VMEM = pl.BlockSpec(memory_space=pltpu.VMEM)


def filter_steps(count, row_shift, segments, even_odd, out, ready, first_turns=2):
    for step in range(1, CHEB + 1):
        low = REACH * step
        turns = first_turns if step == 1 else 2
        unroll = (count - 2 * low) // turns

        def body(turn, step=step, low=low, unroll=unroll):
            for part in range(unroll):
                for which, (facts, base, tiles, first) in enumerate(segments):
                    even, odd = even_odd[which]
                    source = first if step == 1 else (odd if step % 2 == 0 else even)
                    target = odd if step % 2 else even
                    before = first if step == 2 else target
                    block = low + turn * unroll + part
                    row = block - row_shift
                    left = jnp.concatenate([tiles[row, t] for t in range(4)], axis=1)
                    right = jnp.concatenate([source[facts[base + row, t]] for t in range(4)], axis=0)
                    value = jnp.dot(left, right, preferred_element_type=F32)
                    value = value * facts[base + row, 4].astype(F32)
                    if step > 1:
                        value = 2.0 * value - before[block].astype(F32)
                    if step == CHEB:
                        out[which * (count - 2 * low) + turn * unroll + part] = value.astype(BF)
                    else:
                        target[block] = value.astype(BF)

        if step == 1 and ready is not None:
            for turn in range(turns):
                ready(turn)
                body(turn)
        else:

            def looped(turn, carry, body=body):
                body(turn)
                return carry

            lax.fori_loop(0, turns, looped, 0)


def inner_kernel(count, facts, tiles, vectors, out, seg_t, seg_v, even, odd, sems):
    copies = []

    def copy(source, target, begin, end):
        at = pl.ds(begin, end - begin)
        copies.append(pltpu.make_async_copy(source.at[at], target.at[at], sems.at[len(copies)]))
        copies[-1].start()

    turns = 4
    per_turn = (count - 2 * REACH) // turns
    ends = [REACH + per_turn * (turn + 1) for turn in range(turns - 1)] + [count]
    middle = ends[1] + REACH
    copy(vectors, seg_v, 0, middle)
    for turn in range(turns):
        if turn == 2:
            copy(vectors, seg_v, middle, count)
        copy(tiles, seg_t, ends[turn - 1] if turn else 0, ends[turn])

    def ready(turn):
        for copied in {0: copies[0:2], 1: copies[2:3], 2: copies[3:5], 3: copies[5:6]}[turn]:
            copied.wait()

    filter_steps(count, 0, [(facts, 0, seg_t, seg_v)], [(even, odd)], out, ready, turns)


def edge_kernel(count, facts, core, tiles, vectors, near, far, vlow, vhigh,
                out, seg_v, seg_t, even, odd, even1, odd1, sems):
    deep_rows = DEEP - REACH
    span = 3 * DEEP
    c = core[0]
    own_rows = 2 * DEEP - REACH
    copies = []

    def copy(source, target):
        copies.append(pltpu.make_async_copy(source, target, sems.at[len(copies)]))
        copies[-1].start()

    moved = deep_rows * 4
    for segment, halo, near_v, far_v, far_t in (
        (0, vlow, 0, DEEP, deep_rows),
        (1, vhigh, 2 * DEEP, 0, 0),
    ):
        own_v = 0 if segment == 0 else count - 2 * DEEP
        own_t = 0 if segment == 0 else count - own_rows
        copy(halo.at[pl.ds(0, DEEP)], seg_v.at[segment, pl.ds(near_v, DEEP)])
        copy(vectors.at[pl.ds(own_v, 2 * DEEP)], seg_v.at[segment, pl.ds(far_v, 2 * DEEP)])
        copy(
            tiles.at[pl.ds(own_t * 4, own_rows * 4)],
            seg_t.at[segment, pl.ds(far_t * 4, own_rows * 4)],
        )
    copy(near, seg_t.at[c, pl.ds(c * (own_rows * 4), moved)])
    copy(far, seg_t.at[1 - c, pl.ds((1 - c) * (own_rows * 4), moved)])
    for c in copies:
        c.wait()

    class Rows:
        def __init__(self, which):
            self.which = which

        def __getitem__(self, at):
            return seg_t[self.which, at[0] * 4 + at[1]]

    filter_steps(
        span,
        REACH,
        [
            (facts, 0, Rows(0), seg_v.at[0]),
            (facts, span - 2 * REACH, Rows(1), seg_v.at[1]),
        ],
        [(even, odd), (even1, odd1)],
        out,
        None,
    )


def gram_kernel(half, with_base, place, *refs):
    if with_base:
        base, refs = refs[0], refs[1:]
    own_in, twin_in, n1, s1, o1, os1, out, flipped, own, twin, beside, across, sems = refs
    i, c = place[2], place[3]
    copies = []

    def copy(source, target):
        copies.append(pltpu.make_async_copy(source, target, sems.at[len(copies)]))
        copies[-1].start()

    copy(own_in, own)
    copy(twin_in, twin)
    for e in range(2):
        copy(n1.at[e], beside.at[c, e])
        copy(s1.at[1 - e], beside.at[1 - c, e])
        copy(o1.at[e], across.at[c, e])
        copy(os1.at[1 - e], across.at[1 - c, e])
    for copied in copies:
        copied.wait()
    q = half // 2
    for part in range(4):
        flipped[part] = own[part * q : (part + 1) * q, :].T

    def dot(part, piece):
        return jnp.dot(flipped[part], piece, preferred_element_type=F32)

    def all_rows(piece):
        return sum(dot(p, piece[p * q : (p + 1) * q]) for p in range(4)) * 0.5

    values = [all_rows(own), all_rows(twin)]
    for e in range(2):
        values.append(dot(0, beside[0, e, :q]) + dot(1, beside[0, e, q:]))
    for e in range(2):
        values.append(dot(i, across[0, e]) + dot(2 + i, across[1, e]))
    for e in range(2):
        values.append(dot(2, beside[1, e, :q]) + dot(3, beside[1, e, q:]))
    for column, value in enumerate(values):
        if with_base:
            value = value + base[:, column * 128 : (column + 1) * 128]
        out[:, column * 128 : (column + 1) * 128] = value.astype(out.dtype)


def split(value):
    high = value.astype(BF)
    return high, (value - high.astype(F32)).astype(BF)


def final_kernel(place, scale_in, gathered, gathered_twin, *refs):
    pieces, (out, rows_buf, table, matrix, sems) = refs[:16], refs[16:]
    x, y, i, c = place[0], place[1], place[2], place[3]
    low = DEEP * 128
    total = rows_buf.shape[1]
    inner = (total - 2 * low) // 2
    copies = [[], []]

    def copy(group, source, row, count, panel):
        copied = pltpu.make_async_copy(
            source, rows_buf.at[panel, pl.ds(row, count)], sems.at[len(copies[0]) + len(copies[1])]
        )
        copied.start()
        copies[group].append(copied)

    n2, s2, o2, os2 = pieces[12:16]
    groups = ((low, low + inner, inner, 0), (0, low + 2 * inner, low, inner))
    for group, (first, second, half, at) in enumerate(groups):
        m2, t2, skip = ((n2, s2, 0), (o2, os2, inner + low))[group]
        own, twin, n1, s1, o1, os1 = pieces[6 * group : 6 * group + 6]
        q = half // 2
        step = c * (second - first)
        up, down = first + step, second - step
        for e, piece in enumerate((own, twin)):
            copy(group, piece.at[pl.ds(0, half)], first, half, e)
            copy(group, piece.at[pl.ds(half, half)], second, half, e)
        for e in range(2):
            mine, other = i * q, (1 - i) * q
            copy(group, n1.at[e], up, half, 2 + e + 4 * c)
            copy(group, s1.at[1 - e], down, half, 6 + e - 4 * c)
            copy(group, o1.at[e], up + mine, q, 4 + e)
            copy(group, os1.at[1 - e], down + mine, q, 4 + e)
            copy(group, m2.at[pl.ds(skip + e * half, half)], down, half, 2 + e + 4 * c)
            copy(group, t2.at[pl.ds(skip + (1 - e) * half, half)], up, half, 6 + e - 4 * c)
            copy(group, o2.at[pl.ds(at + e * q, q)], up + other, q, 4 + e)
            copy(group, os2.at[pl.ds(at + (1 - e) * q, q)], down + other, q, 4 + e)

    for dx in range(4):
        for dy in range(4):
            chunk = lax.rem(x + dx, 4) * 4 + lax.rem(y + dy, 4)
            for dz in range(4):
                for e in range(2):
                    piece = (gathered_twin if e else gathered)[(dx * 4 + dy) * 4 + dz].astype(F32)
                    for qz in range(4):
                        for qe in range(2):
                            column = 2 * ((dz + qz) % 4) + (e ^ qe)
                            table[2 * dz + e, chunk, :, pl.ds(column * 128, 128)] = piece[
                                :, (2 * qz + qe) * 128 : (2 * qz + qe + 1) * 128
                            ]
    width = 1024
    diagonal = lax.broadcasted_iota(jnp.int32, (128, 128), 0) == lax.broadcasted_iota(
        jnp.int32, (128, 128), 1
    )
    eye = diagonal.astype(F32)
    trace = jnp.zeros((128, 128), F32)
    for p in range(8):
        panel = table[p].reshape(128, width)
        matrix[pl.ds(p * 128, 128), :] = panel.astype(BF)
        trace = trace + panel[:, p * 128 : (p + 1) * 128] * eye
    mean = 2.0 * jnp.sum(trace) / float(total * 16)
    scale = scale_in[0] * mean / width
    kappa = 1.0 / (scale * float(total * 16))
    own_row = table[0].reshape(128, width)
    own_column = jnp.concatenate(
        [table[p].reshape(128, width)[:, 0:128].T for p in range(8)], axis=1
    )
    unit = jnp.concatenate([eye, jnp.zeros((128, width - 128), F32)], axis=1)
    root = 1.5 * unit - (0.5 * kappa) * (own_row + own_column)

    def times(value):
        both = jnp.concatenate(split(value), axis=0)
        whole = matrix[...]
        product = jnp.dot(both, whole, preferred_element_type=F32) + lax.dot_general(
            both, whole, (((1,), (1,)), ((), ())), preferred_element_type=F32
        )
        return kappa * (product[:128] + product[128:])

    second = 1.5 * root - 0.5 * times(root)
    third = 1.5 * second - 0.5 * times(second)
    result = 1.5 * root - 0.5 * times(third)
    weights = (result / jnp.sqrt(jnp.full((128, width), scale, F32))).astype(BF).T
    step = 512
    ranges = ([(low, low + 2 * inner)], [(0, low), (low + 2 * inner, total)])
    for group in range(2):
        for copied in copies[group]:
            copied.wait()
        for begin, end in ranges[group]:
            for row in range(begin, end, step):
                left = jnp.concatenate([rows_buf[p, row : row + step] for p in range(8)], axis=1)
                product = jnp.dot(left, weights, preferred_element_type=F32)
                out[row : row + step] = product.astype(BF)


def params(limit):
    return pltpu.CompilerParams(vmem_limit_bytes=limit * 2**20)


def cost(flops, data):
    return pl.CostEstimate(flops=flops, bytes_accessed=data, transcendentals=0)


def local(ham_tiles, tile_columns, stack_lengths, start_vectors, spectral_scale):
    row_count, panel = start_vectors.shape
    blocks = ham_tiles.shape[0]
    total_blocks = blocks * lax.axis_size("row")
    row_at, vec_at = lax.axis_index("row"), lax.axis_index("vec")
    z_at, core_at = vec_at // 2, vec_at % 2
    rows16, zs = lax.axis_size("row"), lax.axis_size("vec") // 2

    def z_perm(move, flip=0):
        return [
            (2 * z + c, 2 * ((z + move) % zs) + (c ^ flip)) for z in range(zs) for c in range(2)
        ]

    def by_z(value, move):
        return lax.ppermute(value, "vec", z_perm(move))

    def swap(value):
        return lax.ppermute(value, "vec", z_perm(0, 1))

    forward = [(r, (r + 1) % rows16) for r in range(rows16)]
    backward = [(r, (r - 1) % rows16) for r in range(rows16)]

    block_ids = row_at * blocks + jnp.arange(blocks, dtype=jnp.int32)
    offsets = (tile_columns - block_ids[:, None] + REACH) % total_blocks - REACH
    local_rows = jnp.arange(blocks, dtype=jnp.int32)
    live = ((local_rows < stack_lengths[0] - REACH) | (local_rows >= blocks - REACH)).astype(
        jnp.int32
    )
    meta = jnp.concatenate([offsets, jnp.broadcast_to(live[:, None], (blocks, 4))], axis=1)
    vectors = start_vectors.reshape(blocks, 128, panel)
    flat_tiles = ham_tiles.reshape(blocks * 4, 128, 128)
    deep_rows = DEEP - REACH

    devices = [(r, z, c) for r in range(rows16) for z in range(zs) for c in range(2)]
    row_sides = [
        ((r * zs + z) * 2 + c, ((r + 1 - 2 * c) % rows16 * zs + z) * 2 + c) for r, z, c in devices
    ]
    sides = [(2 * z + c, 2 * ((z - 1 + 2 * c) % zs) + c) for z in range(zs) for c in range(2)]

    def with_facts(part, facts):
        block = jnp.pad(facts.astype(BF), ((0, 128 - deep_rows), (0, 120)))[None]
        return jnp.concatenate([part, block], axis=0)

    near = lax.ppermute(
        lax.dynamic_slice_in_dim(
            flat_tiles, (1 - core_at) * (4 * (blocks - deep_rows)), 4 * deep_rows, 0
        ),
        ("row", "vec"),
        row_sides,
    )
    vlow = lax.ppermute(
        with_facts(vectors[blocks - DEEP :], meta[blocks - deep_rows :]), "row", forward
    )
    vhigh = lax.ppermute(with_facts(vectors[:DEEP], meta[:deep_rows]), "row", backward)
    near, vlow, vhigh = lax.optimization_barrier((near, vlow, vhigh))
    far = swap(near)
    meta_low = vlow[-1, :deep_rows, :8].astype(jnp.int32)
    meta_high = vhigh[-1, :deep_rows, :8].astype(jnp.int32)

    inner_blocks = blocks - 2 * DEEP
    places = (jnp.arange(8) < 4).astype(jnp.int32)[None, :]
    inner_facts = meta + places * local_rows[:, None]
    inner = pl.pallas_call(
        functools.partial(inner_kernel, blocks),
        out_shape=jax.ShapeDtypeStruct((inner_blocks, 128, panel), BF),
        in_specs=[SMEM, ANY, ANY],
        out_specs=VMEM,
        scratch_shapes=[
            pltpu.VMEM((blocks, 4, 128, 128), BF),
            pltpu.VMEM((blocks, 128, panel), BF),
            pltpu.VMEM((blocks, 128, panel), BF),
            pltpu.VMEM((blocks, 128, panel), BF),
            pltpu.SemaphoreType.DMA((6,)),
        ],
        compiler_params=params(58),
        cost_estimate=cost(10**6, 2**20),
        name="inner_filter",
    )(inner_facts, ham_tiles, vectors)

    own_rows = 2 * DEEP - REACH
    edge_facts = jnp.concatenate(
        [meta_low, meta[:own_rows], meta[blocks - own_rows :], meta_high], axis=0
    )
    edge_facts = edge_facts + places * (
        REACH + jnp.arange(2 * (own_rows + deep_rows), dtype=jnp.int32) % (own_rows + deep_rows)
    )[:, None]
    inner_own = inner.reshape(inner_blocks * 128, panel)

    quarter_of = jnp.where(z_at < 2, 0, 1).astype(jnp.int32)
    send_left = jnp.where((z_at + zs - 1) % zs < 2, 0, 1).astype(jnp.int32)
    send_right = jnp.where((z_at + 1) % zs < 2, 0, 1).astype(jnp.int32)

    place = jnp.stack([row_at // 4, row_at % 4, quarter_of, core_at]).astype(jnp.int32)
    forward_part = jnp.where(core_at == 0, send_left, send_right)

    def half_of(value, which):
        h = value.shape[0] // 2
        return lax.dynamic_slice_in_dim(value, which * h, h, 0)

    def pieces_of(pair_value, which):
        h = pair_value.shape[0] // 2
        q = h // 2
        return [lax.dynamic_slice_in_dim(pair_value, e * h + which * q, q, 0) for e in range(2)]

    def join(parts):
        return jnp.concatenate(parts, axis=0)

    def by_side(value):
        return lax.ppermute(value, "vec", sides)

    def send_near(own, before_twin, before):
        early, *_ = lax.optimization_barrier((own, *before_twin))
        twin = swap(early)
        sent, *_ = lax.optimization_barrier(
            (join([half_of(own, core_at), half_of(twin, core_at)]), *before)
        )
        return own, twin, sent, by_side(sent)

    def rest_of(own, twin):
        return join([half_of(own, 1 - core_at), half_of(twin, 1 - core_at)])

    def two(value):
        return value.reshape(2, value.shape[0] // 2, panel)

    def gram(got, base):
        args = list(got[:2]) + [two(v) for v in got[2:]]
        half = got[0].shape[0] // 2
        return pl.pallas_call(
            functools.partial(gram_kernel, half, base is not None),
            out_shape=jax.ShapeDtypeStruct((128, 1024), F32 if base is None else BF),
            in_specs=[SMEM] + [VMEM] * (base is not None) + [ANY] * len(args),
            out_specs=VMEM,
            scratch_shapes=[
                pltpu.VMEM((4, 128, half // 2), BF),
                pltpu.VMEM((2 * half, panel), BF),
                pltpu.VMEM((2 * half, panel), BF),
                pltpu.VMEM((2, 2, half, panel), BF),
                pltpu.VMEM((2, 2, half // 2, panel), BF),
                pltpu.SemaphoreType.DMA((10,)),
            ],
            compiler_params=params(56),
            cost_estimate=cost(half * 256 * 1024, half * 128 * 24),
            name="gram",
        )(place, *([base] if base is not None else []), *args)

    own, twin, _, n1 = send_near(inner_own, (near, vlow, vhigh), (far,))
    inner_near = [own, twin, n1, swap(n1), by_side(join(pieces_of(n1, forward_part)))]
    core_arg = core_at.astype(jnp.int32)[None]
    edge = pl.pallas_call(
        functools.partial(edge_kernel, blocks),
        out_shape=jax.ShapeDtypeStruct((2 * DEEP, 128, panel), BF),
        in_specs=[SMEM] * 2 + [ANY] * 6,
        out_specs=VMEM,
        scratch_shapes=[
            pltpu.VMEM((2, 3 * DEEP, 128, panel), BF),
            pltpu.VMEM((2, (3 * DEEP - 2 * REACH) * 4, 128, 128), BF),
        ]
        + [pltpu.VMEM((3 * DEEP, 128, panel), BF)] * 4
        + [pltpu.SemaphoreType.DMA((10,))],
        compiler_params=params(58),
        cost_estimate=cost(8 * 10**9, 11 * 2**20),
        name="edge_filter",
    )(edge_facts, core_arg, flat_tiles, vectors, near, far, vlow, vhigh)
    edge_own = edge.reshape(2 * DEEP * 128, panel)
    own, twin, sent, n1 = send_near(edge_own, (), ())
    s1 = swap(n1)
    o1, _ = lax.optimization_barrier((inner_near[4], sent))
    os1 = swap(o1)
    n1_late, os1_early = lax.optimization_barrier((n1, os1))
    os1, _ = lax.optimization_barrier((os1_early, s1))
    inner_got = inner_near[:4] + [o1, os1]
    inner_gram = gram(inner_got, None)
    o1 = by_side(join(pieces_of(n1_late, forward_part)))
    o1_late, _ = lax.optimization_barrier((o1, inner_gram))
    edge_got = [own, twin, n1, s1, o1, swap(o1_late)]
    whole_gram = gram(edge_got, inner_gram)

    late, _ = lax.optimization_barrier(
        (rest_of(*inner_got[:2]), o1_late)
    )
    n2 = by_side(late)

    pieces = lax.all_to_all(
        whole_gram.reshape(rows16, 128 // rows16, 1024), "row", split_axis=0, concat_axis=0
    )
    mine = jnp.sum(pieces.astype(F32), axis=0).astype(BF)[None]
    mine, n2 = lax.optimization_barrier((mine, n2))

    def around(value, axis, perm_of):
        parts = [value] + [lax.ppermute(value, axis, perm_of(d)) for d in (1, 2, 3)]
        return jnp.concatenate(parts, axis=0)

    def row_perm(dx, dy):
        return [
            (4 * a + b, 4 * ((a - dx) % 4) + (b - dy) % 4) for a in range(4) for b in range(4)
        ]

    got = around(mine, "vec", lambda d: z_perm(-d))
    later, _ = lax.optimization_barrier(
        (
            join(
                pieces_of(inner_got[2], 1 - forward_part)
                + pieces_of(edge_got[2], 1 - forward_part)
                + [rest_of(*edge_got[:2])]
            ),
            got,
        )
    )
    o2 = by_side(later)
    got = around(got, "row", lambda d: row_perm(0, d))
    got = around(got, "row", lambda d: row_perm(d, 0))
    parts = []
    for values in (inner_got, edge_got):
        parts += list(values[:2]) + [two(v) for v in values[2:]]
    o2_late, _ = lax.optimization_barrier((o2, got))
    parts += [n2, swap(n2), o2, swap(o2_late)]
    return pl.pallas_call(
        final_kernel,
        out_shape=jax.ShapeDtypeStruct((row_count, panel), BF),
        in_specs=[SMEM, SMEM, VMEM, VMEM] + [ANY] * len(parts),
        out_specs=VMEM,
        scratch_shapes=[
            pltpu.VMEM((8, row_count, 128), BF),
            pltpu.VMEM((8, rows16, 128 // rows16, 1024), F32),
            pltpu.VMEM((1024, 1024), BF),
            pltpu.SemaphoreType.DMA((40,)),
        ],
        compiler_params=params(58),
        cost_estimate=cost(6 * 10**9, 20 * 2**20),
        name="final",
    )(place, spectral_scale, got, swap(got), *parts)


def solution(mesh):
    placed = (P("row", None, None, None), P("row", None), P("row"), P("row", "vec"), P())
    return jax.shard_map(
        local, mesh=mesh, in_specs=placed, out_specs=P("row", "vec"), check_vma=False
    )
```

```python
import functools

import jax
import jax.numpy as jnp
from jax import lax
from jax.experimental import pallas as pl
from jax.experimental.pallas import tpu as pltpu
from jax.sharding import PartitionSpec as P

REACH = 2
CHEB = 6
DEEP = REACH * CHEB
BF = jnp.bfloat16
F32 = jnp.float32
ANY = pl.BlockSpec(memory_space=pl.ANY)
SMEM = pl.BlockSpec(memory_space=pltpu.SMEM)
VMEM = pl.BlockSpec(memory_space=pltpu.VMEM)


def filter_steps(count, row_shift, segments, even_odd, out, ready, first_turns=2):
    for step in range(1, CHEB + 1):
        low = REACH * step
        turns = first_turns if step == 1 else 2
        unroll = (count - 2 * low) // turns

        def body(turn, step=step, low=low, unroll=unroll):
            for part in range(unroll):
                for which, (facts, base, tiles, first) in enumerate(segments):
                    even, odd = even_odd[which]
                    source = first if step == 1 else (odd if step % 2 == 0 else even)
                    target = odd if step % 2 else even
                    before = first if step == 2 else target
                    block = low + turn * unroll + part
                    row = block - row_shift
                    left = jnp.concatenate([tiles[row, t] for t in range(4)], axis=1)
                    right = jnp.concatenate([source[facts[base + row, t]] for t in range(4)], axis=0)
                    value = jnp.dot(left, right, preferred_element_type=F32)
                    value = value * facts[base + row, 4].astype(F32)
                    if step > 1:
                        value = 2.0 * value - before[block].astype(F32)
                    if step == CHEB:
                        out[which * (count - 2 * low) + turn * unroll + part] = value.astype(BF)
                    else:
                        target[block] = value.astype(BF)

        if step == 1 and ready is not None:
            for turn in range(turns):
                ready(turn)
                body(turn)
        else:

            def looped(turn, carry, body=body):
                body(turn)
                return carry

            lax.fori_loop(0, turns, looped, 0)


def inner_kernel(count, facts, tiles, vectors, out, seg_t, seg_v, even, odd, sems):
    copies = []

    def copy(source, target, begin, end):
        at = pl.ds(begin, end - begin)
        copies.append(pltpu.make_async_copy(source.at[at], target.at[at], sems.at[len(copies)]))
        copies[-1].start()

    turns = 4
    per_turn = (count - 2 * REACH) // turns
    ends = [REACH + per_turn * (turn + 1) for turn in range(turns - 1)] + [count]
    middle = ends[1] + REACH
    copy(vectors, seg_v, 0, middle)
    for turn in range(turns):
        if turn == 2:
            copy(vectors, seg_v, middle, count)
        copy(tiles, seg_t, ends[turn - 1] if turn else 0, ends[turn])

    def ready(turn):
        for copied in {0: copies[0:2], 1: copies[2:3], 2: copies[3:5], 3: copies[5:6]}[turn]:
            copied.wait()

    filter_steps(count, 0, [(facts, 0, seg_t, seg_v)], [(even, odd)], out, ready, turns)


def edge_kernel(count, facts, core, tiles, vectors, near, far, vlow, vhigh,
                out, seg_v, seg_t, even, odd, even1, odd1, sems):
    deep_rows = DEEP - REACH
    span = 3 * DEEP
    c = core[0]
    own_rows = 2 * DEEP - REACH
    copies = []

    def copy(source, target):
        copies.append(pltpu.make_async_copy(source, target, sems.at[len(copies)]))
        copies[-1].start()

    moved = deep_rows * 4
    for segment, halo, near_v, far_v, far_t in (
        (0, vlow, 0, DEEP, deep_rows),
        (1, vhigh, 2 * DEEP, 0, 0),
    ):
        own_v = 0 if segment == 0 else count - 2 * DEEP
        own_t = 0 if segment == 0 else count - own_rows
        copy(halo.at[pl.ds(0, DEEP)], seg_v.at[segment, pl.ds(near_v, DEEP)])
        copy(vectors.at[pl.ds(own_v, 2 * DEEP)], seg_v.at[segment, pl.ds(far_v, 2 * DEEP)])
        copy(
            tiles.at[pl.ds(own_t * 4, own_rows * 4)],
            seg_t.at[segment, pl.ds(far_t * 4, own_rows * 4)],
        )
    copy(near, seg_t.at[c, pl.ds(c * (own_rows * 4), moved)])
    copy(far, seg_t.at[1 - c, pl.ds((1 - c) * (own_rows * 4), moved)])
    for c in copies:
        c.wait()

    class Rows:
        def __init__(self, which):
            self.which = which

        def __getitem__(self, at):
            return seg_t[self.which, at[0] * 4 + at[1]]

    filter_steps(
        span,
        REACH,
        [
            (facts, 0, Rows(0), seg_v.at[0]),
            (facts, span - 2 * REACH, Rows(1), seg_v.at[1]),
        ],
        [(even, odd), (even1, odd1)],
        out,
        None,
    )


def gram_kernel(half, with_base, place, *refs):
    if with_base:
        base, refs = refs[0], refs[1:]
    own_in, twin_in, n1, s1, o1, os1, out, flipped, own, twin, beside, across, sems = refs
    i, c = place[2], place[3]
    copies = []

    def copy(source, target):
        copies.append(pltpu.make_async_copy(source, target, sems.at[len(copies)]))
        copies[-1].start()

    copy(own_in, own)
    copy(twin_in, twin)
    for e in range(2):
        copy(n1.at[e], beside.at[c, e])
        copy(s1.at[1 - e], beside.at[1 - c, e])
        copy(o1.at[e], across.at[c, e])
        copy(os1.at[1 - e], across.at[1 - c, e])
    for copied in copies:
        copied.wait()
    q = half // 2
    for part in range(4):
        flipped[part] = own[part * q : (part + 1) * q, :].T

    def dot(part, piece):
        return jnp.dot(flipped[part], piece, preferred_element_type=F32)

    def all_rows(piece):
        return sum(dot(p, piece[p * q : (p + 1) * q]) for p in range(4)) * 0.5

    values = [all_rows(own), all_rows(twin)]
    for e in range(2):
        values.append(dot(0, beside[0, e, :q]) + dot(1, beside[0, e, q:]))
    for e in range(2):
        values.append(dot(i, across[0, e]) + dot(2 + i, across[1, e]))
    for e in range(2):
        values.append(dot(2, beside[1, e, :q]) + dot(3, beside[1, e, q:]))
    for column, value in enumerate(values):
        if with_base:
            value = value + base[:, column * 128 : (column + 1) * 128]
        out[:, column * 128 : (column + 1) * 128] = value.astype(out.dtype)


def split(value):
    high = value.astype(BF)
    return high, (value - high.astype(F32)).astype(BF)


def final_kernel(place, scale_in, gathered, gathered_twin, *refs):
    pieces, (out, rows_buf, table, matrix, sems) = refs[:18], refs[18:]
    x, y, i, c = place[0], place[1], place[2], place[3]
    low = DEEP * 128
    total = rows_buf.shape[1]
    inner = (total - 2 * low) // 2
    copies = [[], []]

    def copy(group, source, row, count, panel):
        copied = pltpu.make_async_copy(
            source, rows_buf.at[panel, pl.ds(row, count)], sems.at[len(copies[0]) + len(copies[1])]
        )
        copied.start()
        copies[group].append(copied)

    o2, os2 = pieces[16:18]
    groups = ((low, low + inner, inner, 0), (0, low + 2 * inner, low, inner))
    for group, (first, second, half, at) in enumerate(groups):
        m2, t2 = pieces[12 + 2 * group : 14 + 2 * group]
        own, twin, n1, s1, o1, os1 = pieces[6 * group : 6 * group + 6]
        q = half // 2
        step = c * (second - first)
        up, down = first + step, second - step
        for e, piece in enumerate((own, twin)):
            copy(group, piece.at[pl.ds(0, half)], first, half, e)
            copy(group, piece.at[pl.ds(half, half)], second, half, e)
        for e in range(2):
            mine, other = i * q, (1 - i) * q
            copy(group, n1.at[e], up, half, 2 + e + 4 * c)
            copy(group, s1.at[1 - e], down, half, 6 + e - 4 * c)
            copy(group, o1.at[e], up + mine, q, 4 + e)
            copy(group, os1.at[1 - e], down + mine, q, 4 + e)
            copy(group, m2.at[pl.ds(e * half, half)], down, half, 2 + e + 4 * c)
            copy(group, t2.at[pl.ds((1 - e) * half, half)], up, half, 6 + e - 4 * c)
            copy(group, o2.at[pl.ds(at + e * q, q)], up + other, q, 4 + e)
            copy(group, os2.at[pl.ds(at + (1 - e) * q, q)], down + other, q, 4 + e)

    for dx in range(4):
        for dy in range(4):
            chunk = lax.rem(x + dx, 4) * 4 + lax.rem(y + dy, 4)
            for dz in range(4):
                for e in range(2):
                    piece = (gathered_twin if e else gathered)[(dx * 4 + dy) * 4 + dz].astype(F32)
                    for qz in range(4):
                        for qe in range(2):
                            column = 2 * ((dz + qz) % 4) + (e ^ qe)
                            table[2 * dz + e, chunk, :, pl.ds(column * 128, 128)] = piece[
                                :, (2 * qz + qe) * 128 : (2 * qz + qe + 1) * 128
                            ]
    width = 1024
    diagonal = lax.broadcasted_iota(jnp.int32, (128, 128), 0) == lax.broadcasted_iota(
        jnp.int32, (128, 128), 1
    )
    eye = diagonal.astype(F32)
    trace = jnp.zeros((128, 128), F32)
    for p in range(8):
        panel = table[p].reshape(128, width)
        matrix[pl.ds(p * 128, 128), :] = panel.astype(BF)
        trace = trace + panel[:, p * 128 : (p + 1) * 128] * eye
    mean = 2.0 * jnp.sum(trace) / float(total * 16)
    scale = scale_in[0] * mean / width
    kappa = 1.0 / (scale * float(total * 16))
    own_row = table[0].reshape(128, width)
    own_column = jnp.concatenate(
        [table[p].reshape(128, width)[:, 0:128].T for p in range(8)], axis=1
    )
    unit = jnp.concatenate([eye, jnp.zeros((128, width - 128), F32)], axis=1)
    root = 1.5 * unit - (0.5 * kappa) * (own_row + own_column)

    def times(value):
        both = jnp.concatenate(split(value), axis=0)
        whole = matrix[...]
        product = jnp.dot(both, whole, preferred_element_type=F32) + lax.dot_general(
            both, whole, (((1,), (1,)), ((), ())), preferred_element_type=F32
        )
        return kappa * (product[:128] + product[128:])

    second = 1.5 * root - 0.5 * times(root)
    third = 1.5 * second - 0.5 * times(second)
    result = 1.5 * root - 0.5 * times(third)
    weights = (result / jnp.sqrt(jnp.full((128, width), scale, F32))).astype(BF).T
    step = 512
    ranges = ([(low, low + 2 * inner)], [(0, low), (low + 2 * inner, total)])
    for group in range(2):
        for copied in copies[group]:
            copied.wait()
        for begin, end in ranges[group]:
            for row in range(begin, end, step):
                left = jnp.concatenate([rows_buf[p, row : row + step] for p in range(8)], axis=1)
                product = jnp.dot(left, weights, preferred_element_type=F32)
                out[row : row + step] = product.astype(BF)


def params(limit):
    return pltpu.CompilerParams(vmem_limit_bytes=limit * 2**20)


def cost(flops, data):
    return pl.CostEstimate(flops=flops, bytes_accessed=data, transcendentals=0)


def local(ham_tiles, tile_columns, stack_lengths, start_vectors, spectral_scale):
    row_count, panel = start_vectors.shape
    blocks = ham_tiles.shape[0]
    total_blocks = blocks * lax.axis_size("row")
    row_at, vec_at = lax.axis_index("row"), lax.axis_index("vec")
    z_at, core_at = vec_at // 2, vec_at % 2
    rows16, zs = lax.axis_size("row"), lax.axis_size("vec") // 2

    def z_perm(move, flip=0):
        return [
            (2 * z + c, 2 * ((z + move) % zs) + (c ^ flip)) for z in range(zs) for c in range(2)
        ]

    def by_z(value, move):
        return lax.ppermute(value, "vec", z_perm(move))

    def swap(value):
        return lax.ppermute(value, "vec", z_perm(0, 1))

    forward = [(r, (r + 1) % rows16) for r in range(rows16)]
    backward = [(r, (r - 1) % rows16) for r in range(rows16)]

    block_ids = row_at * blocks + jnp.arange(blocks, dtype=jnp.int32)
    offsets = (tile_columns - block_ids[:, None] + REACH) % total_blocks - REACH
    local_rows = jnp.arange(blocks, dtype=jnp.int32)
    live = ((local_rows < stack_lengths[0] - REACH) | (local_rows >= blocks - REACH)).astype(
        jnp.int32
    )
    meta = jnp.concatenate([offsets, jnp.broadcast_to(live[:, None], (blocks, 4))], axis=1)
    vectors = start_vectors.reshape(blocks, 128, panel)
    flat_tiles = ham_tiles.reshape(blocks * 4, 128, 128)
    deep_rows = DEEP - REACH

    devices = [(r, z, c) for r in range(rows16) for z in range(zs) for c in range(2)]
    row_sides = [
        ((r * zs + z) * 2 + c, ((r + 1 - 2 * c) % rows16 * zs + z) * 2 + c) for r, z, c in devices
    ]
    sides = [(2 * z + c, 2 * ((z - 1 + 2 * c) % zs) + c) for z in range(zs) for c in range(2)]

    def with_facts(part, facts):
        block = jnp.pad(facts.astype(BF), ((0, 128 - deep_rows), (0, 120)))[None]
        return jnp.concatenate([part, block], axis=0)

    near = lax.ppermute(
        lax.dynamic_slice_in_dim(
            flat_tiles, (1 - core_at) * (4 * (blocks - deep_rows)), 4 * deep_rows, 0
        ),
        ("row", "vec"),
        row_sides,
    )
    vlow = lax.ppermute(
        with_facts(vectors[blocks - DEEP :], meta[blocks - deep_rows :]), "row", forward
    )
    vhigh = lax.ppermute(with_facts(vectors[:DEEP], meta[:deep_rows]), "row", backward)
    near, vlow, vhigh = lax.optimization_barrier((near, vlow, vhigh))
    far = swap(near)
    meta_low = vlow[-1, :deep_rows, :8].astype(jnp.int32)
    meta_high = vhigh[-1, :deep_rows, :8].astype(jnp.int32)

    inner_blocks = blocks - 2 * DEEP
    places = (jnp.arange(8) < 4).astype(jnp.int32)[None, :]
    inner_facts = meta + places * local_rows[:, None]
    inner = pl.pallas_call(
        functools.partial(inner_kernel, blocks),
        out_shape=jax.ShapeDtypeStruct((inner_blocks, 128, panel), BF),
        in_specs=[SMEM, ANY, ANY],
        out_specs=VMEM,
        scratch_shapes=[
            pltpu.VMEM((blocks, 4, 128, 128), BF),
            pltpu.VMEM((blocks, 128, panel), BF),
            pltpu.VMEM((blocks, 128, panel), BF),
            pltpu.VMEM((blocks, 128, panel), BF),
            pltpu.SemaphoreType.DMA((6,)),
        ],
        compiler_params=params(58),
        cost_estimate=cost(10**6, 2**20),
        name="inner_filter",
    )(inner_facts, ham_tiles, vectors)

    own_rows = 2 * DEEP - REACH
    edge_facts = jnp.concatenate(
        [meta_low, meta[:own_rows], meta[blocks - own_rows :], meta_high], axis=0
    )
    edge_facts = edge_facts + places * (
        REACH + jnp.arange(2 * (own_rows + deep_rows), dtype=jnp.int32) % (own_rows + deep_rows)
    )[:, None]
    inner_own = inner.reshape(inner_blocks * 128, panel)

    quarter_of = jnp.where(z_at < 2, 0, 1).astype(jnp.int32)
    send_left = jnp.where((z_at + zs - 1) % zs < 2, 0, 1).astype(jnp.int32)
    send_right = jnp.where((z_at + 1) % zs < 2, 0, 1).astype(jnp.int32)

    place = jnp.stack([row_at // 4, row_at % 4, quarter_of, core_at]).astype(jnp.int32)
    forward_part = jnp.where(core_at == 0, send_left, send_right)

    def half_of(value, which):
        h = value.shape[0] // 2
        return lax.dynamic_slice_in_dim(value, which * h, h, 0)

    def pieces_of(pair_value, which):
        h = pair_value.shape[0] // 2
        q = h // 2
        return [lax.dynamic_slice_in_dim(pair_value, e * h + which * q, q, 0) for e in range(2)]

    def join(parts):
        return jnp.concatenate(parts, axis=0)

    def by_side(value):
        return lax.ppermute(value, "vec", sides)

    def send_near(own, before_twin, before):
        early, *_ = lax.optimization_barrier((own, *before_twin))
        twin = swap(early)
        sent, *_ = lax.optimization_barrier(
            (join([half_of(own, core_at), half_of(twin, core_at)]), *before)
        )
        return own, twin, sent, by_side(sent)

    def rest_of(own, twin):
        return join([half_of(own, 1 - core_at), half_of(twin, 1 - core_at)])

    def two(value):
        return value.reshape(2, value.shape[0] // 2, panel)

    def gram(got, base):
        args = list(got[:2]) + [two(v) for v in got[2:]]
        half = got[0].shape[0] // 2
        return pl.pallas_call(
            functools.partial(gram_kernel, half, base is not None),
            out_shape=jax.ShapeDtypeStruct((128, 1024), F32 if base is None else BF),
            in_specs=[SMEM] + [VMEM] * (base is not None) + [ANY] * len(args),
            out_specs=VMEM,
            scratch_shapes=[
                pltpu.VMEM((4, 128, half // 2), BF),
                pltpu.VMEM((2 * half, panel), BF),
                pltpu.VMEM((2 * half, panel), BF),
                pltpu.VMEM((2, 2, half, panel), BF),
                pltpu.VMEM((2, 2, half // 2, panel), BF),
                pltpu.SemaphoreType.DMA((10,)),
            ],
            compiler_params=params(56),
            cost_estimate=cost(half * 256 * 1024, half * 128 * 24),
            name="gram",
        )(place, *([base] if base is not None else []), *args)

    own, twin, sent, n1 = send_near(inner_own, (near, vlow, vhigh), (far,))
    late, _ = lax.optimization_barrier((rest_of(own, twin), sent))
    n2 = by_side(late)
    n1_late, n2 = lax.optimization_barrier((n1, n2))
    s2 = swap(n2)
    inner_near = [own, twin, n1, swap(n1), by_side(join(pieces_of(n1_late, forward_part)))]
    core_arg = core_at.astype(jnp.int32)[None]
    edge = pl.pallas_call(
        functools.partial(edge_kernel, blocks),
        out_shape=jax.ShapeDtypeStruct((2 * DEEP, 128, panel), BF),
        in_specs=[SMEM] * 2 + [ANY] * 6,
        out_specs=VMEM,
        scratch_shapes=[
            pltpu.VMEM((2, 3 * DEEP, 128, panel), BF),
            pltpu.VMEM((2, (3 * DEEP - 2 * REACH) * 4, 128, 128), BF),
        ]
        + [pltpu.VMEM((3 * DEEP, 128, panel), BF)] * 4
        + [pltpu.SemaphoreType.DMA((10,))],
        compiler_params=params(58),
        cost_estimate=cost(8 * 10**9, 11 * 2**20),
        name="edge_filter",
    )(edge_facts, core_arg, flat_tiles, vectors, near, far, vlow, vhigh)
    edge_own = edge.reshape(2 * DEEP * 128, panel)
    own, twin, sent, n1 = send_near(edge_own, (), ())
    s1 = swap(n1)
    o1, _ = lax.optimization_barrier((inner_near[4], sent))
    os1 = swap(o1)
    n1_late, os1_early = lax.optimization_barrier((n1, os1))
    os1, _, s2 = lax.optimization_barrier((os1_early, s1, s2))
    inner_got = inner_near[:4] + [o1, os1]
    inner_gram = gram(inner_got, None)
    o1 = by_side(join(pieces_of(n1_late, forward_part)))
    o1_late, _ = lax.optimization_barrier((o1, inner_gram))
    edge_got = [own, twin, n1, s1, o1, swap(o1_late)]
    whole_gram = gram(edge_got, inner_gram)

    late, _ = lax.optimization_barrier((rest_of(*edge_got[:2]), o1_late))
    edge_n2 = by_side(late)
    edge_s2 = swap(edge_n2)

    pieces = lax.all_to_all(
        whole_gram.reshape(rows16, 128 // rows16, 1024), "row", split_axis=0, concat_axis=0
    )
    mine = jnp.sum(pieces.astype(F32), axis=0).astype(BF)[None]
    mine, edge_n2 = lax.optimization_barrier((mine, edge_n2))

    def around(value, axis, perm_of):
        parts = [value] + [lax.ppermute(value, axis, perm_of(d)) for d in (1, 2, 3)]
        return jnp.concatenate(parts, axis=0)

    def row_perm(dx, dy):
        return [
            (4 * a + b, 4 * ((a - dx) % 4) + (b - dy) % 4) for a in range(4) for b in range(4)
        ]

    got = around(mine, "vec", lambda d: z_perm(-d))
    later, _ = lax.optimization_barrier(
        (
            join(
                pieces_of(inner_got[2], 1 - forward_part)
                + pieces_of(edge_got[2], 1 - forward_part)
            ),
            got,
        )
    )
    o2 = by_side(later)
    got = around(got, "row", lambda d: row_perm(0, d))
    got, edge_s2 = lax.optimization_barrier((got, edge_s2))
    got = around(got, "row", lambda d: row_perm(d, 0))
    parts = []
    for values in (inner_got, edge_got):
        parts += list(values[:2]) + [two(v) for v in values[2:]]
    o2_late, _ = lax.optimization_barrier((o2, got))
    parts += [n2, s2, edge_n2, edge_s2, o2, swap(o2_late)]
    return pl.pallas_call(
        final_kernel,
        out_shape=jax.ShapeDtypeStruct((row_count, panel), BF),
        in_specs=[SMEM, SMEM, VMEM, VMEM] + [ANY] * len(parts),
        out_specs=VMEM,
        scratch_shapes=[
            pltpu.VMEM((8, row_count, 128), BF),
            pltpu.VMEM((8, rows16, 128 // rows16, 1024), F32),
            pltpu.VMEM((1024, 1024), BF),
            pltpu.SemaphoreType.DMA((40,)),
        ],
        compiler_params=params(58),
        cost_estimate=cost(6 * 10**9, 20 * 2**20),
        name="final",
    )(place, spectral_scale, got, swap(got), *parts)


def solution(mesh):
    placed = (P("row", None, None, None), P("row", None), P("row"), P("row", "vec"), P())
    return jax.shard_map(
        local, mesh=mesh, in_specs=placed, out_specs=P("row", "vec"), check_vma=False
    )
```

```python
import functools

import jax
import jax.numpy as jnp
from jax import lax
from jax.experimental import pallas as pl
from jax.experimental.pallas import tpu as pltpu
from jax.sharding import PartitionSpec as P

REACH = 2
CHEB = 6
DEEP = REACH * CHEB
BF = jnp.bfloat16
F32 = jnp.float32
ANY = pl.BlockSpec(memory_space=pl.ANY)
SMEM = pl.BlockSpec(memory_space=pltpu.SMEM)
VMEM = pl.BlockSpec(memory_space=pltpu.VMEM)


def filter_steps(count, row_shift, segments, even_odd, out, ready, first_turns=2):
    for step in range(1, CHEB + 1):
        low = REACH * step
        turns = first_turns if step == 1 else 2
        unroll = (count - 2 * low) // turns

        def body(turn, step=step, low=low, unroll=unroll):
            for part in range(unroll):
                for which, (facts, base, tiles, first) in enumerate(segments):
                    even, odd = even_odd[which]
                    source = first if step == 1 else (odd if step % 2 == 0 else even)
                    target = odd if step % 2 else even
                    before = first if step == 2 else target
                    block = low + turn * unroll + part
                    row = block - row_shift
                    left = jnp.concatenate([tiles[row, t] for t in range(4)], axis=1)
                    right = jnp.concatenate([source[facts[base + row, t]] for t in range(4)], axis=0)
                    value = jnp.dot(left, right, preferred_element_type=F32)
                    value = value * facts[base + row, 4].astype(F32)
                    if step > 1:
                        value = 2.0 * value - before[block].astype(F32)
                    if step == CHEB:
                        out[which * (count - 2 * low) + turn * unroll + part] = value.astype(BF)
                    else:
                        target[block] = value.astype(BF)

        if step == 1 and ready is not None:
            for turn in range(turns):
                ready(turn)
                body(turn)
        else:

            def looped(turn, carry, body=body):
                body(turn)
                return carry

            lax.fori_loop(0, turns, looped, 0)


def inner_kernel(count, facts, tiles, vectors, out, seg_t, seg_v, even, odd, sems):
    copies = []

    def copy(source, target, begin, end):
        at = pl.ds(begin, end - begin)
        copies.append(pltpu.make_async_copy(source.at[at], target.at[at], sems.at[len(copies)]))
        copies[-1].start()

    turns = 4
    per_turn = (count - 2 * REACH) // turns
    ends = [REACH + per_turn * (turn + 1) for turn in range(turns - 1)] + [count]
    middle = ends[1] + REACH
    copy(vectors, seg_v, 0, middle)
    for turn in range(turns):
        if turn == 2:
            copy(vectors, seg_v, middle, count)
        copy(tiles, seg_t, ends[turn - 1] if turn else 0, ends[turn])

    def ready(turn):
        for copied in {0: copies[0:2], 1: copies[2:3], 2: copies[3:5], 3: copies[5:6]}[turn]:
            copied.wait()

    filter_steps(count, 0, [(facts, 0, seg_t, seg_v)], [(even, odd)], out, ready, turns)


def edge_kernel(count, facts, core, tiles, vectors, near, far, vlow, vhigh,
                out, seg_v, seg_t, even, odd, even1, odd1, sems):
    deep_rows = DEEP - REACH
    span = 3 * DEEP
    c = core[0]
    own_rows = 2 * DEEP - REACH
    copies = []

    def copy(source, target):
        copies.append(pltpu.make_async_copy(source, target, sems.at[len(copies)]))
        copies[-1].start()

    moved = deep_rows * 4
    for segment, halo, near_v, far_v, far_t in (
        (0, vlow, 0, DEEP, deep_rows),
        (1, vhigh, 2 * DEEP, 0, 0),
    ):
        own_v = 0 if segment == 0 else count - 2 * DEEP
        own_t = 0 if segment == 0 else count - own_rows
        copy(halo.at[pl.ds(0, DEEP)], seg_v.at[segment, pl.ds(near_v, DEEP)])
        copy(vectors.at[pl.ds(own_v, 2 * DEEP)], seg_v.at[segment, pl.ds(far_v, 2 * DEEP)])
        copy(
            tiles.at[pl.ds(own_t * 4, own_rows * 4)],
            seg_t.at[segment, pl.ds(far_t * 4, own_rows * 4)],
        )
    copy(near, seg_t.at[c, pl.ds(c * (own_rows * 4), moved)])
    copy(far, seg_t.at[1 - c, pl.ds((1 - c) * (own_rows * 4), moved)])
    for c in copies:
        c.wait()

    class Rows:
        def __init__(self, which):
            self.which = which

        def __getitem__(self, at):
            return seg_t[self.which, at[0] * 4 + at[1]]

    filter_steps(
        span,
        REACH,
        [
            (facts, 0, Rows(0), seg_v.at[0]),
            (facts, span - 2 * REACH, Rows(1), seg_v.at[1]),
        ],
        [(even, odd), (even1, odd1)],
        out,
        None,
    )


def gram_kernel(half, with_base, place, *refs):
    if with_base:
        base, refs = refs[0], refs[1:]
    own_in, twin_in, n1, s1, o1, os1, out, flipped, own, twin, beside, across, sems = refs
    i, c = place[2], place[3]
    copies = []

    def copy(source, target):
        copies.append(pltpu.make_async_copy(source, target, sems.at[len(copies)]))
        copies[-1].start()

    copy(own_in, own)
    copy(twin_in, twin)
    for e in range(2):
        copy(n1.at[e], beside.at[c, e])
        copy(s1.at[1 - e], beside.at[1 - c, e])
        copy(o1.at[e], across.at[c, e])
        copy(os1.at[1 - e], across.at[1 - c, e])
    for copied in copies:
        copied.wait()
    q = half // 2
    for part in range(4):
        flipped[part] = own[part * q : (part + 1) * q, :].T

    def dot(part, piece):
        return jnp.dot(flipped[part], piece, preferred_element_type=F32)

    def all_rows(piece):
        return sum(dot(p, piece[p * q : (p + 1) * q]) for p in range(4)) * 0.5

    values = [all_rows(own), all_rows(twin)]
    for e in range(2):
        values.append(dot(0, beside[0, e, :q]) + dot(1, beside[0, e, q:]))
    for e in range(2):
        values.append(dot(i, across[0, e]) + dot(2 + i, across[1, e]))
    for e in range(2):
        values.append(dot(2, beside[1, e, :q]) + dot(3, beside[1, e, q:]))
    for column, value in enumerate(values):
        if with_base:
            value = value + base[:, column * 128 : (column + 1) * 128]
        out[:, column * 128 : (column + 1) * 128] = value.astype(out.dtype)


def split(value):
    high = value.astype(BF)
    return high, (value - high.astype(F32)).astype(BF)


def final_kernel(place, scale_in, gathered, gathered_twin, *refs):
    pieces, (out, rows_buf, table, matrix, sems) = refs[:16], refs[16:]
    x, y, i, c = place[0], place[1], place[2], place[3]
    low = DEEP * 128
    total = rows_buf.shape[1]
    inner = (total - 2 * low) // 2
    copies = [[], []]

    def copy(group, source, row, count, panel):
        copied = pltpu.make_async_copy(
            source, rows_buf.at[panel, pl.ds(row, count)], sems.at[len(copies[0]) + len(copies[1])]
        )
        copied.start()
        copies[group].append(copied)

    n2, s2, o2, os2 = pieces[12:16]
    groups = ((low, low + inner, inner, 0), (0, low + 2 * inner, low, inner))
    for group, (first, second, half, at) in enumerate(groups):
        m2, t2, skip = ((n2, s2, 0), (o2, os2, inner + low))[group]
        own, twin, n1, s1, o1, os1 = pieces[6 * group : 6 * group + 6]
        q = half // 2
        step = c * (second - first)
        up, down = first + step, second - step
        for e, piece in enumerate((own, twin)):
            copy(group, piece.at[pl.ds(0, half)], first, half, e)
            copy(group, piece.at[pl.ds(half, half)], second, half, e)
        for e in range(2):
            mine, other = i * q, (1 - i) * q
            copy(group, n1.at[e], up, half, 2 + e + 4 * c)
            copy(group, s1.at[1 - e], down, half, 6 + e - 4 * c)
            copy(group, o1.at[e], up + mine, q, 4 + e)
            copy(group, os1.at[1 - e], down + mine, q, 4 + e)
            copy(group, m2.at[pl.ds(skip + e * half, half)], down, half, 2 + e + 4 * c)
            copy(group, t2.at[pl.ds(skip + (1 - e) * half, half)], up, half, 6 + e - 4 * c)
            copy(group, o2.at[pl.ds(at + e * q, q)], up + other, q, 4 + e)
            copy(group, os2.at[pl.ds(at + (1 - e) * q, q)], down + other, q, 4 + e)

    for dx in range(4):
        for dy in range(4):
            chunk = lax.rem(x + dx, 4) * 4 + lax.rem(y + dy, 4)
            for dz in range(4):
                for e in range(2):
                    piece = (gathered_twin if e else gathered)[(dx * 4 + dy) * 4 + dz].astype(F32)
                    for qz in range(4):
                        for qe in range(2):
                            column = 2 * ((dz + qz) % 4) + (e ^ qe)
                            table[2 * dz + e, chunk, :, pl.ds(column * 128, 128)] = piece[
                                :, (2 * qz + qe) * 128 : (2 * qz + qe + 1) * 128
                            ]
    width = 1024
    diagonal = lax.broadcasted_iota(jnp.int32, (128, 128), 0) == lax.broadcasted_iota(
        jnp.int32, (128, 128), 1
    )
    eye = diagonal.astype(F32)
    trace = jnp.zeros((128, 128), F32)
    for p in range(8):
        panel = table[p].reshape(128, width)
        matrix[pl.ds(p * 128, 128), :] = panel.astype(BF)
        trace = trace + panel[:, p * 128 : (p + 1) * 128] * eye
    mean = 2.0 * jnp.sum(trace) / float(total * 16)
    scale = scale_in[0] * mean / width
    kappa = 1.0 / (scale * float(total * 16))
    own_row = table[0].reshape(128, width)
    own_column = jnp.concatenate(
        [table[p].reshape(128, width)[:, 0:128].T for p in range(8)], axis=1
    )
    unit = jnp.concatenate([eye, jnp.zeros((128, width - 128), F32)], axis=1)
    root = 1.5 * unit - (0.5 * kappa) * (own_row + own_column)

    def times(value):
        both = jnp.concatenate(split(value), axis=0)
        whole = matrix[...]
        product = jnp.dot(both, whole, preferred_element_type=F32) + lax.dot_general(
            both, whole, (((1,), (1,)), ((), ())), preferred_element_type=F32
        )
        return kappa * (product[:128] + product[128:])

    second = 1.5 * root - 0.5 * times(root)
    third = 1.5 * second - 0.5 * times(second)
    result = 1.5 * root - 0.5 * times(third)
    weights = (result / jnp.sqrt(jnp.full((128, width), scale, F32))).astype(BF).T
    step = 512
    ranges = ([(low, low + 2 * inner)], [(0, low), (low + 2 * inner, total)])
    for group in range(2):
        for copied in copies[group]:
            copied.wait()
        for begin, end in ranges[group]:
            for row in range(begin, end, step):
                left = jnp.concatenate([rows_buf[p, row : row + step] for p in range(8)], axis=1)
                product = jnp.dot(left, weights, preferred_element_type=F32)
                out[row : row + step] = product.astype(BF)


def params(limit):
    return pltpu.CompilerParams(vmem_limit_bytes=limit * 2**20)


def cost(flops, data):
    return pl.CostEstimate(flops=flops, bytes_accessed=data, transcendentals=0)


def local(ham_tiles, tile_columns, stack_lengths, start_vectors, spectral_scale):
    row_count, panel = start_vectors.shape
    blocks = ham_tiles.shape[0]
    total_blocks = blocks * lax.axis_size("row")
    row_at, vec_at = lax.axis_index("row"), lax.axis_index("vec")
    z_at, core_at = vec_at // 2, vec_at % 2
    rows16, zs = lax.axis_size("row"), lax.axis_size("vec") // 2

    def z_perm(move, flip=0):
        return [
            (2 * z + c, 2 * ((z + move) % zs) + (c ^ flip)) for z in range(zs) for c in range(2)
        ]

    def by_z(value, move):
        return lax.ppermute(value, "vec", z_perm(move))

    def swap(value):
        return lax.ppermute(value, "vec", z_perm(0, 1))

    forward = [(r, (r + 1) % rows16) for r in range(rows16)]
    backward = [(r, (r - 1) % rows16) for r in range(rows16)]

    block_ids = row_at * blocks + jnp.arange(blocks, dtype=jnp.int32)
    offsets = (tile_columns - block_ids[:, None] + REACH) % total_blocks - REACH
    local_rows = jnp.arange(blocks, dtype=jnp.int32)
    live = ((local_rows < stack_lengths[0] - REACH) | (local_rows >= blocks - REACH)).astype(
        jnp.int32
    )
    meta = jnp.concatenate([offsets, jnp.broadcast_to(live[:, None], (blocks, 4))], axis=1)
    vectors = start_vectors.reshape(blocks, 128, panel)
    flat_tiles = ham_tiles.reshape(blocks * 4, 128, 128)
    deep_rows = DEEP - REACH

    devices = [(r, z, c) for r in range(rows16) for z in range(zs) for c in range(2)]
    row_sides = [
        ((r * zs + z) * 2 + c, ((r + 1 - 2 * c) % rows16 * zs + z) * 2 + c) for r, z, c in devices
    ]
    sides = [(2 * z + c, 2 * ((z - 1 + 2 * c) % zs) + c) for z in range(zs) for c in range(2)]

    def with_facts(part, facts):
        block = jnp.pad(facts.astype(BF), ((0, 128 - deep_rows), (0, 120)))[None]
        return jnp.concatenate([part, block], axis=0)

    near = lax.ppermute(
        lax.dynamic_slice_in_dim(
            flat_tiles, (1 - core_at) * (4 * (blocks - deep_rows)), 4 * deep_rows, 0
        ),
        ("row", "vec"),
        row_sides,
    )
    vlow = lax.ppermute(
        with_facts(vectors[blocks - DEEP :], meta[blocks - deep_rows :]), "row", forward
    )
    vhigh = lax.ppermute(with_facts(vectors[:DEEP], meta[:deep_rows]), "row", backward)
    near, vlow, vhigh = lax.optimization_barrier((near, vlow, vhigh))
    far = swap(near)
    meta_low = vlow[-1, :deep_rows, :8].astype(jnp.int32)
    meta_high = vhigh[-1, :deep_rows, :8].astype(jnp.int32)

    inner_blocks = blocks - 2 * DEEP
    places = (jnp.arange(8) < 4).astype(jnp.int32)[None, :]
    inner_facts = meta + places * local_rows[:, None]
    inner = pl.pallas_call(
        functools.partial(inner_kernel, blocks),
        out_shape=jax.ShapeDtypeStruct((inner_blocks, 128, panel), BF),
        in_specs=[SMEM, ANY, ANY],
        out_specs=VMEM,
        scratch_shapes=[
            pltpu.VMEM((blocks, 4, 128, 128), BF),
            pltpu.VMEM((blocks, 128, panel), BF),
            pltpu.VMEM((blocks, 128, panel), BF),
            pltpu.VMEM((blocks, 128, panel), BF),
            pltpu.SemaphoreType.DMA((6,)),
        ],
        compiler_params=params(58),
        cost_estimate=cost(10**6, 2**20),
        name="inner_filter",
    )(inner_facts, ham_tiles, vectors)

    own_rows = 2 * DEEP - REACH
    edge_facts = jnp.concatenate(
        [meta_low, meta[:own_rows], meta[blocks - own_rows :], meta_high], axis=0
    )
    edge_facts = edge_facts + places * (
        REACH + jnp.arange(2 * (own_rows + deep_rows), dtype=jnp.int32) % (own_rows + deep_rows)
    )[:, None]
    inner_own = inner.reshape(inner_blocks * 128, panel)

    quarter_of = jnp.where(z_at < 2, 0, 1).astype(jnp.int32)
    send_left = jnp.where((z_at + zs - 1) % zs < 2, 0, 1).astype(jnp.int32)
    send_right = jnp.where((z_at + 1) % zs < 2, 0, 1).astype(jnp.int32)

    place = jnp.stack([row_at // 4, row_at % 4, quarter_of, core_at]).astype(jnp.int32)
    forward_part = jnp.where(core_at == 0, send_left, send_right)

    def half_of(value, which):
        h = value.shape[0] // 2
        return lax.dynamic_slice_in_dim(value, which * h, h, 0)

    def pieces_of(pair_value, which):
        h = pair_value.shape[0] // 2
        q = h // 2
        return [lax.dynamic_slice_in_dim(pair_value, e * h + which * q, q, 0) for e in range(2)]

    def join(parts):
        return jnp.concatenate(parts, axis=0)

    def by_side(value):
        return lax.ppermute(value, "vec", sides)

    def send_near(own, before_twin, before):
        early, *_ = lax.optimization_barrier((own, *before_twin))
        twin = swap(early)
        sent, *_ = lax.optimization_barrier(
            (join([half_of(own, core_at), half_of(twin, core_at)]), *before)
        )
        return own, twin, sent, by_side(sent)

    def rest_of(own, twin):
        return join([half_of(own, 1 - core_at), half_of(twin, 1 - core_at)])

    def two(value):
        return value.reshape(2, value.shape[0] // 2, panel)

    def gram(got, base):
        args = list(got[:2]) + [two(v) for v in got[2:]]
        half = got[0].shape[0] // 2
        return pl.pallas_call(
            functools.partial(gram_kernel, half, base is not None),
            out_shape=jax.ShapeDtypeStruct((128, 1024), F32 if base is None else BF),
            in_specs=[SMEM] + [VMEM] * (base is not None) + [ANY] * len(args),
            out_specs=VMEM,
            scratch_shapes=[
                pltpu.VMEM((4, 128, half // 2), BF),
                pltpu.VMEM((2 * half, panel), BF),
                pltpu.VMEM((2 * half, panel), BF),
                pltpu.VMEM((2, 2, half, panel), BF),
                pltpu.VMEM((2, 2, half // 2, panel), BF),
                pltpu.SemaphoreType.DMA((10,)),
            ],
            compiler_params=params(56),
            cost_estimate=cost(half * 256 * 1024, half * 128 * 24),
            name="gram",
        )(place, *([base] if base is not None else []), *args)

    own, twin, _, n1 = send_near(inner_own, (near, vlow, vhigh), (far,))
    inner_near = [own, twin, n1, swap(n1), by_side(join(pieces_of(n1, forward_part)))]
    core_arg = core_at.astype(jnp.int32)[None]
    edge = pl.pallas_call(
        functools.partial(edge_kernel, blocks),
        out_shape=jax.ShapeDtypeStruct((2 * DEEP, 128, panel), BF),
        in_specs=[SMEM] * 2 + [ANY] * 6,
        out_specs=VMEM,
        scratch_shapes=[
            pltpu.VMEM((2, 3 * DEEP, 128, panel), BF),
            pltpu.VMEM((2, (3 * DEEP - 2 * REACH) * 4, 128, 128), BF),
        ]
        + [pltpu.VMEM((3 * DEEP, 128, panel), BF)] * 4
        + [pltpu.SemaphoreType.DMA((10,))],
        compiler_params=params(58),
        cost_estimate=cost(8 * 10**9, 11 * 2**20),
        name="edge_filter",
    )(edge_facts, core_arg, flat_tiles, vectors, near, far, vlow, vhigh)
    edge_own = edge.reshape(2 * DEEP * 128, panel)
    own, twin, sent, n1 = send_near(edge_own, (), ())
    s1 = swap(n1)
    o1, _ = lax.optimization_barrier((inner_near[4], sent))
    os1 = swap(o1)
    n1_late, os1_early = lax.optimization_barrier((n1, os1))
    os1, _ = lax.optimization_barrier((os1_early, s1))
    inner_got = inner_near[:4] + [o1, os1]
    inner_gram = gram(inner_got, None)
    o1 = by_side(join(pieces_of(n1_late, forward_part)))
    o1_late, _ = lax.optimization_barrier((o1, inner_gram))
    edge_got = [own, twin, n1, s1, o1, swap(o1_late)]
    whole_gram = gram(edge_got, inner_gram)

    late, _ = lax.optimization_barrier(
        (rest_of(*inner_got[:2]), o1_late)
    )
    n2 = by_side(late)

    pieces = lax.all_to_all(
        whole_gram.reshape(rows16, 128 // rows16, 1024), "row", split_axis=0, concat_axis=0
    )
    mine = jnp.sum(pieces.astype(F32), axis=0).astype(BF)[None]
    mine, n2 = lax.optimization_barrier((mine, n2))

    def around(value, axis, perm_of):
        parts = [value] + [lax.ppermute(value, axis, perm_of(d)) for d in (1, 2, 3)]
        return jnp.concatenate(parts, axis=0)

    def row_perm(dx, dy):
        return [
            (4 * a + b, 4 * ((a - dx) % 4) + (b - dy) % 4) for a in range(4) for b in range(4)
        ]

    got = around(mine, "vec", lambda d: z_perm(-d))
    later, _ = lax.optimization_barrier(
        (
            join(
                pieces_of(inner_got[2], 1 - forward_part)
                + pieces_of(edge_got[2], 1 - forward_part)
                + [rest_of(*edge_got[:2])]
            ),
            got,
        )
    )
    o2 = by_side(later)
    got = around(got, "row", lambda d: row_perm(0, d))
    got, s2 = lax.optimization_barrier((got, swap(n2)))
    got = around(got, "row", lambda d: row_perm(d, 0))
    parts = []
    for values in (inner_got, edge_got):
        parts += list(values[:2]) + [two(v) for v in values[2:]]
    o2_late, _ = lax.optimization_barrier((o2, got))
    parts += [n2, s2, o2, swap(o2_late)]
    return pl.pallas_call(
        final_kernel,
        out_shape=jax.ShapeDtypeStruct((row_count, panel), BF),
        in_specs=[SMEM, SMEM, VMEM, VMEM] + [ANY] * len(parts),
        out_specs=VMEM,
        scratch_shapes=[
            pltpu.VMEM((8, row_count, 128), BF),
            pltpu.VMEM((8, rows16, 128 // rows16, 1024), F32),
            pltpu.VMEM((1024, 1024), BF),
            pltpu.SemaphoreType.DMA((40,)),
        ],
        compiler_params=params(58),
        cost_estimate=cost(6 * 10**9, 20 * 2**20),
        name="final",
    )(place, spectral_scale, got, swap(got), *parts)


def solution(mesh):
    placed = (P("row", None, None, None), P("row", None), P("row"), P("row", "vec"), P())
    return jax.shard_map(
        local, mesh=mesh, in_specs=placed, out_specs=P("row", "vec"), check_vma=False
    )
```

```python
import functools

import jax
import jax.numpy as jnp
from jax import lax
from jax.experimental import pallas as pl
from jax.experimental.pallas import tpu as pltpu
from jax.sharding import PartitionSpec as P

REACH = 2
CHEB = 6
DEEP = REACH * CHEB
BF = jnp.bfloat16
F32 = jnp.float32
ANY = pl.BlockSpec(memory_space=pl.ANY)
SMEM = pl.BlockSpec(memory_space=pltpu.SMEM)
VMEM = pl.BlockSpec(memory_space=pltpu.VMEM)


def filter_steps(count, row_shift, segments, even_odd, out, ready, first_turns=2):
    for step in range(1, CHEB + 1):
        low = REACH * step
        turns = first_turns if step == 1 else 2
        unroll = (count - 2 * low) // turns

        def body(turn, step=step, low=low, unroll=unroll):
            for part in range(unroll):
                for which, (facts, base, tiles, first) in enumerate(segments):
                    even, odd = even_odd[which]
                    source = first if step == 1 else (odd if step % 2 == 0 else even)
                    target = odd if step % 2 else even
                    before = first if step == 2 else target
                    block = low + turn * unroll + part
                    row = block - row_shift
                    left = jnp.concatenate([tiles[row, t] for t in range(4)], axis=1)
                    right = jnp.concatenate([source[facts[base + row, t]] for t in range(4)], axis=0)
                    value = jnp.dot(left, right, preferred_element_type=F32)
                    value = value * facts[base + row, 4].astype(F32)
                    if step > 1:
                        value = 2.0 * value - before[block].astype(F32)
                    if step == CHEB:
                        out[which * (count - 2 * low) + turn * unroll + part] = value.astype(BF)
                    else:
                        target[block] = value.astype(BF)

        if step == 1 and ready is not None:
            for turn in range(turns):
                ready(turn)
                body(turn)
        else:

            def looped(turn, carry, body=body):
                body(turn)
                return carry

            lax.fori_loop(0, turns, looped, 0)


def inner_kernel(count, facts, tiles, vectors, out, seg_t, seg_v, even, odd, sems):
    copies = []

    def copy(source, target, begin, end):
        at = pl.ds(begin, end - begin)
        copies.append(pltpu.make_async_copy(source.at[at], target.at[at], sems.at[len(copies)]))
        copies[-1].start()

    turns = 4
    per_turn = (count - 2 * REACH) // turns
    ends = [REACH + per_turn * (turn + 1) for turn in range(turns - 1)] + [count]
    middle = ends[1] + REACH
    copy(vectors, seg_v, 0, middle)
    for turn in range(turns):
        if turn == 2:
            copy(vectors, seg_v, middle, count)
        copy(tiles, seg_t, ends[turn - 1] if turn else 0, ends[turn])

    def ready(turn):
        for copied in {0: copies[0:2], 1: copies[2:3], 2: copies[3:5], 3: copies[5:6]}[turn]:
            copied.wait()

    filter_steps(count, 0, [(facts, 0, seg_t, seg_v)], [(even, odd)], out, ready, turns)


def edge_kernel(count, facts, core, tiles, vectors, near, far, vlow, vhigh,
                out, seg_v, seg_t, even, odd, even1, odd1, sems):
    deep_rows = DEEP - REACH
    span = 3 * DEEP
    c = core[0]
    own_rows = 2 * DEEP - REACH
    copies = []

    def copy(source, target):
        copies.append(pltpu.make_async_copy(source, target, sems.at[len(copies)]))
        copies[-1].start()

    moved = deep_rows * 4
    for segment, halo, near_v, far_v, far_t in (
        (0, vlow, 0, DEEP, deep_rows),
        (1, vhigh, 2 * DEEP, 0, 0),
    ):
        own_v = 0 if segment == 0 else count - 2 * DEEP
        own_t = 0 if segment == 0 else count - own_rows
        copy(halo.at[pl.ds(0, DEEP)], seg_v.at[segment, pl.ds(near_v, DEEP)])
        copy(vectors.at[pl.ds(own_v, 2 * DEEP)], seg_v.at[segment, pl.ds(far_v, 2 * DEEP)])
        soon = (span // 2 - REACH - far_t) * 4
        for begin, end in ((0, soon), (soon, own_rows * 4)):
            copy(
                tiles.at[pl.ds(own_t * 4 + begin, end - begin)],
                seg_t.at[segment, pl.ds(far_t * 4 + begin, end - begin)],
            )
    copy(near, seg_t.at[c, pl.ds(c * (own_rows * 4), moved)])
    copy(far, seg_t.at[1 - c, pl.ds((1 - c) * (own_rows * 4), moved)])
    order = (copies[:3] + copies[4:7] + copies[8:], (copies[3], copies[7]))

    def ready(turn):
        for copied in order[turn]:
            copied.wait()

    class Rows:
        def __init__(self, which):
            self.which = which

        def __getitem__(self, at):
            return seg_t[self.which, at[0] * 4 + at[1]]

    filter_steps(
        span,
        REACH,
        [
            (facts, 0, Rows(0), seg_v.at[0]),
            (facts, span - 2 * REACH, Rows(1), seg_v.at[1]),
        ],
        [(even, odd), (even1, odd1)],
        out,
        ready,
    )


def gram_kernel(half, with_base, place, *refs):
    if with_base:
        base, refs = refs[0], refs[1:]
    own_in, twin_in, n1, s1, o1, os1, out, flipped, own, twin, beside, across, sems = refs
    i, c = place[2], place[3]
    copies = []

    def copy(source, target):
        copies.append(pltpu.make_async_copy(source, target, sems.at[len(copies)]))
        copies[-1].start()

    copy(own_in, own)
    copy(twin_in, twin)
    for e in range(2):
        copy(n1.at[e], beside.at[c, e])
        copy(s1.at[1 - e], beside.at[1 - c, e])
        copy(o1.at[e], across.at[c, e])
        copy(os1.at[1 - e], across.at[1 - c, e])
    for copied in copies:
        copied.wait()
    q = half // 2
    for part in range(4):
        flipped[part] = own[part * q : (part + 1) * q, :].T

    def dot(part, piece):
        return jnp.dot(flipped[part], piece, preferred_element_type=F32)

    def all_rows(piece):
        return sum(dot(p, piece[p * q : (p + 1) * q]) for p in range(4)) * 0.5

    values = [all_rows(own), all_rows(twin)]
    for e in range(2):
        values.append(dot(0, beside[0, e, :q]) + dot(1, beside[0, e, q:]))
    for e in range(2):
        values.append(dot(i, across[0, e]) + dot(2 + i, across[1, e]))
    for e in range(2):
        values.append(dot(2, beside[1, e, :q]) + dot(3, beside[1, e, q:]))
    for column, value in enumerate(values):
        if with_base:
            value = value + base[:, column * 128 : (column + 1) * 128]
        out[:, column * 128 : (column + 1) * 128] = value.astype(out.dtype)


def split(value):
    high = value.astype(BF)
    return high, (value - high.astype(F32)).astype(BF)


def final_kernel(place, scale_in, gathered, gathered_twin, *refs):
    pieces, (out, rows_buf, table, matrix, sems) = refs[:16], refs[16:]
    x, y, i, c = place[0], place[1], place[2], place[3]
    low = DEEP * 128
    total = rows_buf.shape[1]
    inner = (total - 2 * low) // 2
    copies = [[], []]

    def copy(group, source, row, count, panel):
        copied = pltpu.make_async_copy(
            source, rows_buf.at[panel, pl.ds(row, count)], sems.at[len(copies[0]) + len(copies[1])]
        )
        copied.start()
        copies[group].append(copied)

    n2, s2, o2, os2 = pieces[12:16]
    groups = ((low, low + inner, inner, 0), (0, low + 2 * inner, low, inner))
    for group, (first, second, half, at) in enumerate(groups):
        m2, t2, skip = ((n2, s2, 0), (o2, os2, inner + low))[group]
        own, twin, n1, s1, o1, os1 = pieces[6 * group : 6 * group + 6]
        q = half // 2
        step = c * (second - first)
        up, down = first + step, second - step
        for e, piece in enumerate((own, twin)):
            copy(group, piece.at[pl.ds(0, half)], first, half, e)
            copy(group, piece.at[pl.ds(half, half)], second, half, e)
        for e in range(2):
            mine, other = i * q, (1 - i) * q
            copy(group, n1.at[e], up, half, 2 + e + 4 * c)
            copy(group, s1.at[1 - e], down, half, 6 + e - 4 * c)
            copy(group, o1.at[e], up + mine, q, 4 + e)
            copy(group, os1.at[1 - e], down + mine, q, 4 + e)
            copy(group, m2.at[pl.ds(skip + e * half, half)], down, half, 2 + e + 4 * c)
            copy(group, t2.at[pl.ds(skip + (1 - e) * half, half)], up, half, 6 + e - 4 * c)
            copy(group, o2.at[pl.ds(at + e * q, q)], up + other, q, 4 + e)
            copy(group, os2.at[pl.ds(at + (1 - e) * q, q)], down + other, q, 4 + e)

    for dx in range(4):
        for dy in range(4):
            chunk = lax.rem(x + dx, 4) * 4 + lax.rem(y + dy, 4)
            for dz in range(4):
                for e in range(2):
                    piece = (gathered_twin if e else gathered)[(dx * 4 + dy) * 4 + dz].astype(F32)
                    for qz in range(4):
                        for qe in range(2):
                            column = 2 * ((dz + qz) % 4) + (e ^ qe)
                            table[2 * dz + e, chunk, :, pl.ds(column * 128, 128)] = piece[
                                :, (2 * qz + qe) * 128 : (2 * qz + qe + 1) * 128
                            ]
    width = 1024
    diagonal = lax.broadcasted_iota(jnp.int32, (128, 128), 0) == lax.broadcasted_iota(
        jnp.int32, (128, 128), 1
    )
    eye = diagonal.astype(F32)
    trace = jnp.zeros((128, 128), F32)
    for p in range(8):
        panel = table[p].reshape(128, width)
        matrix[pl.ds(p * 128, 128), :] = panel.astype(BF)
        trace = trace + panel[:, p * 128 : (p + 1) * 128] * eye
    mean = 2.0 * jnp.sum(trace) / float(total * 16)
    scale = scale_in[0] * mean / width
    kappa = 1.0 / (scale * float(total * 16))
    own_row = table[0].reshape(128, width)
    own_column = jnp.concatenate(
        [table[p].reshape(128, width)[:, 0:128].T for p in range(8)], axis=1
    )
    unit = jnp.concatenate([eye, jnp.zeros((128, width - 128), F32)], axis=1)
    root = 1.5 * unit - (0.5 * kappa) * (own_row + own_column)

    def times(value):
        both = jnp.concatenate(split(value), axis=0)
        whole = matrix[...]
        product = jnp.dot(both, whole, preferred_element_type=F32) + lax.dot_general(
            both, whole, (((1,), (1,)), ((), ())), preferred_element_type=F32
        )
        return kappa * (product[:128] + product[128:])

    second = 1.5 * root - 0.5 * times(root)
    third = 1.5 * second - 0.5 * times(second)
    result = 1.5 * root - 0.5 * times(third)
    weights = (result / jnp.sqrt(jnp.full((128, width), scale, F32))).astype(BF).T
    step = 512
    ranges = ([(low, low + 2 * inner)], [(0, low), (low + 2 * inner, total)])
    for group in range(2):
        for copied in copies[group]:
            copied.wait()
        for begin, end in ranges[group]:
            for row in range(begin, end, step):
                left = jnp.concatenate([rows_buf[p, row : row + step] for p in range(8)], axis=1)
                product = jnp.dot(left, weights, preferred_element_type=F32)
                out[row : row + step] = product.astype(BF)


def params(limit):
    return pltpu.CompilerParams(vmem_limit_bytes=limit * 2**20)


def cost(flops, data):
    return pl.CostEstimate(flops=flops, bytes_accessed=data, transcendentals=0)


def local(ham_tiles, tile_columns, stack_lengths, start_vectors, spectral_scale):
    row_count, panel = start_vectors.shape
    blocks = ham_tiles.shape[0]
    total_blocks = blocks * lax.axis_size("row")
    row_at, vec_at = lax.axis_index("row"), lax.axis_index("vec")
    z_at, core_at = vec_at // 2, vec_at % 2
    rows16, zs = lax.axis_size("row"), lax.axis_size("vec") // 2

    def z_perm(move, flip=0):
        return [
            (2 * z + c, 2 * ((z + move) % zs) + (c ^ flip)) for z in range(zs) for c in range(2)
        ]

    def by_z(value, move):
        return lax.ppermute(value, "vec", z_perm(move))

    def swap(value):
        return lax.ppermute(value, "vec", z_perm(0, 1))

    forward = [(r, (r + 1) % rows16) for r in range(rows16)]
    backward = [(r, (r - 1) % rows16) for r in range(rows16)]

    block_ids = row_at * blocks + jnp.arange(blocks, dtype=jnp.int32)
    offsets = (tile_columns - block_ids[:, None] + REACH) % total_blocks - REACH
    local_rows = jnp.arange(blocks, dtype=jnp.int32)
    live = ((local_rows < stack_lengths[0] - REACH) | (local_rows >= blocks - REACH)).astype(
        jnp.int32
    )
    meta = jnp.concatenate([offsets, jnp.broadcast_to(live[:, None], (blocks, 4))], axis=1)
    vectors = start_vectors.reshape(blocks, 128, panel)
    flat_tiles = ham_tiles.reshape(blocks * 4, 128, 128)
    deep_rows = DEEP - REACH

    devices = [(r, z, c) for r in range(rows16) for z in range(zs) for c in range(2)]
    row_sides = [
        ((r * zs + z) * 2 + c, ((r + 1 - 2 * c) % rows16 * zs + z) * 2 + c) for r, z, c in devices
    ]
    sides = [(2 * z + c, 2 * ((z - 1 + 2 * c) % zs) + c) for z in range(zs) for c in range(2)]

    def with_facts(part, facts):
        block = jnp.pad(facts.astype(BF), ((0, 128 - deep_rows), (0, 120)))[None]
        return jnp.concatenate([part, block], axis=0)

    near = lax.ppermute(
        lax.dynamic_slice_in_dim(
            flat_tiles, (1 - core_at) * (4 * (blocks - deep_rows)), 4 * deep_rows, 0
        ),
        ("row", "vec"),
        row_sides,
    )
    vlow = lax.ppermute(
        with_facts(vectors[blocks - DEEP :], meta[blocks - deep_rows :]), "row", forward
    )
    vhigh = lax.ppermute(with_facts(vectors[:DEEP], meta[:deep_rows]), "row", backward)
    near, vlow, vhigh = lax.optimization_barrier((near, vlow, vhigh))
    far = swap(near)
    meta_low = vlow[-1, :deep_rows, :8].astype(jnp.int32)
    meta_high = vhigh[-1, :deep_rows, :8].astype(jnp.int32)

    inner_blocks = blocks - 2 * DEEP
    places = (jnp.arange(8) < 4).astype(jnp.int32)[None, :]
    inner_facts = meta + places * local_rows[:, None]
    inner = pl.pallas_call(
        functools.partial(inner_kernel, blocks),
        out_shape=jax.ShapeDtypeStruct((inner_blocks, 128, panel), BF),
        in_specs=[SMEM, ANY, ANY],
        out_specs=VMEM,
        scratch_shapes=[
            pltpu.VMEM((blocks, 4, 128, 128), BF),
            pltpu.VMEM((blocks, 128, panel), BF),
            pltpu.VMEM((blocks, 128, panel), BF),
            pltpu.VMEM((blocks, 128, panel), BF),
            pltpu.SemaphoreType.DMA((6,)),
        ],
        compiler_params=params(58),
        cost_estimate=cost(10**6, 2**20),
        name="inner_filter",
    )(inner_facts, ham_tiles, vectors)

    own_rows = 2 * DEEP - REACH
    edge_facts = jnp.concatenate(
        [meta_low, meta[:own_rows], meta[blocks - own_rows :], meta_high], axis=0
    )
    edge_facts = edge_facts + places * (
        REACH + jnp.arange(2 * (own_rows + deep_rows), dtype=jnp.int32) % (own_rows + deep_rows)
    )[:, None]
    inner_own = inner.reshape(inner_blocks * 128, panel)

    quarter_of = jnp.where(z_at < 2, 0, 1).astype(jnp.int32)
    send_left = jnp.where((z_at + zs - 1) % zs < 2, 0, 1).astype(jnp.int32)
    send_right = jnp.where((z_at + 1) % zs < 2, 0, 1).astype(jnp.int32)

    place = jnp.stack([row_at // 4, row_at % 4, quarter_of, core_at]).astype(jnp.int32)
    forward_part = jnp.where(core_at == 0, send_left, send_right)

    def half_of(value, which):
        h = value.shape[0] // 2
        return lax.dynamic_slice_in_dim(value, which * h, h, 0)

    def pieces_of(pair_value, which):
        h = pair_value.shape[0] // 2
        q = h // 2
        return [lax.dynamic_slice_in_dim(pair_value, e * h + which * q, q, 0) for e in range(2)]

    def join(parts):
        return jnp.concatenate(parts, axis=0)

    def by_side(value):
        return lax.ppermute(value, "vec", sides)

    def send_near(own, before_twin, before):
        early, *_ = lax.optimization_barrier((own, *before_twin))
        twin = swap(early)
        sent, *_ = lax.optimization_barrier(
            (join([half_of(own, core_at), half_of(twin, core_at)]), *before)
        )
        return own, twin, sent, by_side(sent)

    def rest_of(own, twin):
        return join([half_of(own, 1 - core_at), half_of(twin, 1 - core_at)])

    def two(value):
        return value.reshape(2, value.shape[0] // 2, panel)

    def gram(got, base):
        args = list(got[:2]) + [two(v) for v in got[2:]]
        half = got[0].shape[0] // 2
        return pl.pallas_call(
            functools.partial(gram_kernel, half, base is not None),
            out_shape=jax.ShapeDtypeStruct((128, 1024), F32 if base is None else BF),
            in_specs=[SMEM] + [VMEM] * (base is not None) + [ANY] * len(args),
            out_specs=VMEM,
            scratch_shapes=[
                pltpu.VMEM((4, 128, half // 2), BF),
                pltpu.VMEM((2 * half, panel), BF),
                pltpu.VMEM((2 * half, panel), BF),
                pltpu.VMEM((2, 2, half, panel), BF),
                pltpu.VMEM((2, 2, half // 2, panel), BF),
                pltpu.SemaphoreType.DMA((10,)),
            ],
            compiler_params=params(56),
            cost_estimate=cost(half * 256 * 1024, half * 128 * 24),
            name="gram",
        )(place, *([base] if base is not None else []), *args)

    own, twin, _, n1 = send_near(inner_own, (near, vlow, vhigh), (far,))
    inner_near = [own, twin, n1, swap(n1), by_side(join(pieces_of(n1, forward_part)))]
    core_arg = core_at.astype(jnp.int32)[None]
    edge = pl.pallas_call(
        functools.partial(edge_kernel, blocks),
        out_shape=jax.ShapeDtypeStruct((2 * DEEP, 128, panel), BF),
        in_specs=[SMEM] * 2 + [ANY] * 6,
        out_specs=VMEM,
        scratch_shapes=[
            pltpu.VMEM((2, 3 * DEEP, 128, panel), BF),
            pltpu.VMEM((2, (3 * DEEP - 2 * REACH) * 4, 128, 128), BF),
        ]
        + [pltpu.VMEM((3 * DEEP, 128, panel), BF)] * 4
        + [pltpu.SemaphoreType.DMA((12,))],
        compiler_params=params(58),
        cost_estimate=cost(8 * 10**9, 11 * 2**20),
        name="edge_filter",
    )(edge_facts, core_arg, flat_tiles, vectors, near, far, vlow, vhigh)
    edge_own = edge.reshape(2 * DEEP * 128, panel)
    own, twin, sent, n1 = send_near(edge_own, (), ())
    s1 = swap(n1)
    o1, _ = lax.optimization_barrier((inner_near[4], sent))
    os1 = swap(o1)
    n1_late, os1_early = lax.optimization_barrier((n1, os1))
    os1, _ = lax.optimization_barrier((os1_early, s1))
    inner_got = inner_near[:4] + [o1, os1]
    inner_gram = gram(inner_got, None)
    o1 = by_side(join(pieces_of(n1_late, forward_part)))
    o1_late, _ = lax.optimization_barrier((o1, inner_gram))
    edge_got = [own, twin, n1, s1, o1, swap(o1_late)]
    whole_gram = gram(edge_got, inner_gram)

    late, _ = lax.optimization_barrier(
        (rest_of(*inner_got[:2]), o1_late)
    )
    n2 = by_side(late)

    pieces = lax.all_to_all(
        whole_gram.reshape(rows16, 128 // rows16, 1024), "row", split_axis=0, concat_axis=0
    )
    mine = jnp.sum(pieces.astype(F32), axis=0).astype(BF)[None]
    mine, n2 = lax.optimization_barrier((mine, n2))

    def around(value, axis, perm_of):
        parts = [value] + [lax.ppermute(value, axis, perm_of(d)) for d in (1, 2, 3)]
        return jnp.concatenate(parts, axis=0)

    def row_perm(dx, dy):
        return [
            (4 * a + b, 4 * ((a - dx) % 4) + (b - dy) % 4) for a in range(4) for b in range(4)
        ]

    got = around(mine, "vec", lambda d: z_perm(-d))
    later, _ = lax.optimization_barrier(
        (
            join(
                pieces_of(inner_got[2], 1 - forward_part)
                + pieces_of(edge_got[2], 1 - forward_part)
                + [rest_of(*edge_got[:2])]
            ),
            got,
        )
    )
    o2 = by_side(later)
    got = around(got, "row", lambda d: row_perm(0, d))
    got, s2 = lax.optimization_barrier((got, swap(n2)))
    got = around(got, "row", lambda d: row_perm(d, 0))
    parts = []
    for values in (inner_got, edge_got):
        parts += list(values[:2]) + [two(v) for v in values[2:]]
    o2_late, _ = lax.optimization_barrier((o2, got))
    parts += [n2, s2, o2, swap(o2_late)]
    return pl.pallas_call(
        final_kernel,
        out_shape=jax.ShapeDtypeStruct((row_count, panel), BF),
        in_specs=[SMEM, SMEM, VMEM, VMEM] + [ANY] * len(parts),
        out_specs=VMEM,
        scratch_shapes=[
            pltpu.VMEM((8, row_count, 128), BF),
            pltpu.VMEM((8, rows16, 128 // rows16, 1024), F32),
            pltpu.VMEM((1024, 1024), BF),
            pltpu.SemaphoreType.DMA((40,)),
        ],
        compiler_params=params(58),
        cost_estimate=cost(6 * 10**9, 20 * 2**20),
        name="final",
    )(place, spectral_scale, got, swap(got), *parts)


def solution(mesh):
    placed = (P("row", None, None, None), P("row", None), P("row"), P("row", "vec"), P())
    return jax.shard_map(
        local, mesh=mesh, in_specs=placed, out_specs=P("row", "vec"), check_vma=False
    )
```
